32 devices in a mesh: groups: 2 (over y), row: 4 (over z), col: 4 (over x, core).
Axes of the slice: x: 2, y: 2, z: 4, core: 2. Of those that a mesh axis runs over, the one named last changes fastest.
Arguments:
- b_occ_i: bfloat16 [12, 2048, 6144], P('groups', 'row', 'col'), parts along dimension 0, may hold values from -0.625 to 0.625
- b_occ_j: bfloat16 [4, 2048, 6144], P('groups', 'row', 'col'), parts along dimension 0, may hold values from -0.625 to 0.625
- eps_occ_i: float32 [12], P('groups'), parts along dimension 0, may hold values from -1.5 to -0.4
- eps_occ_j: float32 [4], P('groups'), parts along dimension 0, may hold values from -1.5 to -0.4
- eps_vir: float32 [4096], P('groups'), parts along dimension 0, may hold values from 0.2 to 4
Outputs:
- gamma: float32 [12, 2048, 6144], P('groups', 'row', 'col'), parts along dimension 0
The draws below stay inside these ranges and needn't reach their ends.
There are 2 independent parts, one for each index of `groups`. The reference program is written for one: setup_inputs(seed, part) draws one part's arguments, and reference() takes and returns one part's arrays. A program takes and returns all parts, laid end to end along the dimension named above; each array names one. Nothing has to cross between parts.
All inputs are finite; a program needn't handle non-finite values.
Results may differ from the reference program's by a relative error of at most 0.01.
Values may be sent and summed in bfloat16 or wider, within the bound.
No kernel may reach another device: no remote copies, remote signals or barrier semaphores. Data moves between devices by JAX's collectives and lax.ppermute only.
A program may use at most 320 MiB of HBM per device.

```python
import math
import jax
import jax.numpy as jnp
from jax import lax

A = 2048
NAUX = 6144
OCC_I = 6
OCC_J = 2
N_COL = 4


def steps_of(key, shape, cuts, low, top_value):
    factor_of = 1.0
    for position, parts in cuts:
        heights = jax.random.uniform(jax.random.fold_in(jax.random.fold_in(key, 6), position), (parts,), jnp.float32, low / len(cuts), top_value / len(cuts))
        factor_of = factor_of * jnp.repeat(jnp.exp(heights), shape[position] // parts).reshape((-1,) + (1,) * (len(shape) - 1 - position))
    return factor_of


def scatter_about(rng, shape, scale, bound, pieces=(), held_as=jnp.bfloat16):
    entries = jax.random.normal(rng, shape, jnp.float32) * scale
    if len(pieces) > 0:
        entries = steps_of(rng, shape, pieces, -0.22, 0.18) * entries
    return jnp.clip(entries, min=-bound, max=bound).astype(held_as)


def setup_inputs(seed: int = 0, part: int = 0) -> dict:
    keys = jax.random.split(jax.random.key(seed), 6)
    part_splits = jax.random.split(jax.random.fold_in(keys[5], part), 6)
    b_occ_i = scatter_about(part_splits[0], (OCC_I, A, NAUX), (max(NAUX // 64, 8)) ** -0.5, 0.625, ((1, 4), (2, 4)))
    b_occ_j = scatter_about(part_splits[1], (OCC_J, A, NAUX), (max(NAUX // 64, 8)) ** -0.5, 0.625, ((1, 4), (2, 4)))
    eps_occ_i = jnp.clip(jax.random.uniform(part_splits[2], (OCC_I,), jnp.float32, -1.5, -0.4), -1.5, -0.4)
    eps_occ_j = jnp.clip(jax.random.uniform(part_splits[3], (OCC_J,), jnp.float32, -1.5, -0.4), -1.5, -0.4)
    eps_vir = jnp.clip(jnp.exp(jax.random.uniform(part_splits[4], (A,), jnp.float32, math.log(0.2), math.log(4.0))), 0.2, 4.0)
    return {"b_occ_i": b_occ_i, "b_occ_j": b_occ_j, "eps_occ_i": eps_occ_i, "eps_occ_j": eps_occ_j, "eps_vir": eps_vir}


def reference(b_occ_i, b_occ_j, eps_occ_i, eps_occ_j, eps_vir):
    block = NAUX // N_COL
    flat_i = b_occ_i.reshape(OCC_I * A, NAUX)
    gamma = jnp.zeros((OCC_I, A, NAUX), jnp.float32)
    for orbital in range(OCC_J):
        totals = jnp.zeros((OCC_I * A, A), jnp.float32)
        for block_index in range(N_COL):
            lower = block_index * block
            left = flat_i[:, lower:lower + block]
            right = b_occ_j[orbital, :, lower:lower + block]
            piece = jnp.dot(left, right.T, preferred_element_type=jnp.float32)
            rounded = lax.optimization_barrier(piece.astype(jnp.bfloat16))
            totals = totals + rounded.astype(jnp.float32)
        denominator = (eps_occ_i[:, None, None] + eps_occ_j[orbital]
                       - eps_vir[None, :, None] - eps_vir[None, None, :])
        amplitudes = (totals.reshape(OCC_I, A, A) / denominator).astype(jnp.bfloat16)
        held = lax.optimization_barrier(amplitudes).astype(jnp.float32)
        combined = (2.0 * held - jnp.swapaxes(held, 1, 2)).astype(jnp.bfloat16)
        update = jnp.dot(combined.reshape(OCC_I * A, A), b_occ_j[orbital], preferred_element_type=jnp.float32)
        gamma = gamma + update.reshape(OCC_I, A, NAUX)
    return gamma
```

```python
import functools

import jax
import jax.numpy as jnp
from jax import lax
from jax.experimental import pallas as pl
from jax.experimental.pallas import tpu as pltpu
from jax.sharding import PartitionSpec as P

F32 = jnp.float32
BF16 = jnp.bfloat16
ANY = pl.BlockSpec(memory_space=pl.ANY)
PARAMS = pltpu.CompilerParams(vmem_limit_bytes=48 * 2**20)


def cost(flops, *arrays):
    size = sum(a.size * a.dtype.itemsize for a in arrays)
    return pl.CostEstimate(flops=flops, bytes_accessed=size, transcendentals=0)


def times_transposed(left, right):
    return lax.dot_general(left, right, (((1,), (1,)), ((), ())), preferred_element_type=F32)


def send_kernel(place, b_i, block, out):
    out[0, 0] = times_transposed(b_i[0], block[0]).astype(BF16)


def pairs_for_core(place, b_i, block):
    n_j, cols, depth = block.shape
    half, rows = b_i.shape[0] // 2, b_i.shape[1]
    out = jax.ShapeDtypeStruct((n_j, half, rows, cols), BF16)
    return pl.pallas_call(
        send_kernel,
        out_shape=out,
        grid_spec=pltpu.PrefetchScalarGridSpec(
            num_scalar_prefetch=1,
            grid=(half, n_j),
            in_specs=[
                pl.BlockSpec((1, rows, depth), lambda i, j, s: ((1 - s[1]) * half + i, 0, 0)),
                pl.BlockSpec((1, cols, depth), lambda i, j, s: (j, 0, 0)),
            ],
            out_specs=pl.BlockSpec((1, 1, rows, cols), lambda i, j, s: (j, i, 0, 0)),
        ),
        compiler_params=PARAMS,
        cost_estimate=cost(2 * n_j * half * rows * cols * depth, b_i, block, out),
        name="pairs_for_core",
    )(place, b_i, block)


def chip_kernel(place, b_i, block, core, out):
    out[0] = (times_transposed(b_i[0], block[0]) + core[0, 0].astype(F32)).astype(BF16)


def pairs_for_chip(place, b_i, block, core):
    n_j, cols, depth = block.shape
    half, rows = b_i.shape[0] // 2, b_i.shape[1]
    out = jax.ShapeDtypeStruct((half, rows, cols), BF16)
    return pl.pallas_call(
        chip_kernel,
        out_shape=out,
        grid_spec=pltpu.PrefetchScalarGridSpec(
            num_scalar_prefetch=1,
            grid=(half,),
            in_specs=[
                pl.BlockSpec((1, rows, depth), lambda i, s: (s[1] * half + i, 0, 0)),
                pl.BlockSpec((1, cols, depth), lambda i, s: (1 - s[0], 0, 0)),
                pl.BlockSpec((1, 1, rows, cols), lambda i, s: (1 - s[0], i, 0, 0)),
            ],
            out_specs=pl.BlockSpec((1, rows, cols), lambda i, s: (i, 0, 0)),
        ),
        compiler_params=PARAMS,
        cost_estimate=cost(2 * half * rows * cols * depth, out, out, out),
        name="pairs_for_chip",
    )(place, b_i, block, core)


def own_kernel(place, occ, b_i, block, core, chip, vir_a, vir_b, out):
    total = times_transposed(b_i[0], block[0]) + core[0, 0].astype(F32) + chip[0].astype(F32)
    denominator = (occ[pl.program_id(0)] - vir_a[...]) - vir_b[...]
    out[0] = (total / denominator).astype(BF16)


def own_amplitudes(place, occ, b_i, block, core, chip, vir_a, vir_b):
    n_j, cols, depth = block.shape
    half, rows = b_i.shape[0] // 2, b_i.shape[1]
    out = jax.ShapeDtypeStruct((half, rows, cols), BF16)
    return pl.pallas_call(
        own_kernel,
        out_shape=out,
        grid_spec=pltpu.PrefetchScalarGridSpec(
            num_scalar_prefetch=2,
            grid=(half,),
            in_specs=[
                pl.BlockSpec((1, rows, depth), lambda i, s, o: (s[1] * half + i, 0, 0)),
                pl.BlockSpec((1, cols, depth), lambda i, s, o: (s[0], 0, 0)),
                pl.BlockSpec((1, 1, rows, cols), lambda i, s, o: (s[0], i, 0, 0)),
                pl.BlockSpec((1, rows, cols), lambda i, s, o: (i, 0, 0)),
                pl.BlockSpec((rows, 1), lambda i, s, o: (0, 0)),
                pl.BlockSpec((1, cols), lambda i, s, o: (0, 0)),
            ],
            out_specs=pl.BlockSpec((1, rows, cols), lambda i, s, o: (i, 0, 0)),
        ),
        compiler_params=PARAMS,
        cost_estimate=cost(2 * half * rows * cols * depth, out, out, out),
        name="own_amplitudes",
    )(place, occ, b_i, block, core, chip, vir_a, vir_b)


def combine_kernel(held, mirror, out):
    out[0] = (2.0 * held[0].astype(F32) - mirror[0].astype(F32).T).astype(BF16)


def combine_pairs(held, mirror):
    spec = pl.BlockSpec((1,) + held.shape[1:], lambda i: (i, 0, 0))
    return pl.pallas_call(
        combine_kernel,
        out_shape=jax.ShapeDtypeStruct(held.shape, BF16),
        grid=(held.shape[0],),
        in_specs=[spec, spec],
        out_specs=spec,
        compiler_params=PARAMS,
        cost_estimate=cost(0, held, mirror, held),
        name="combine_pairs",
    )(held, mirror)


def gamma_kernel(has_sum, place, same_j, other_j, block, *rest):
    x = place[0]
    total = jnp.dot(same_j[0], block[x], preferred_element_type=F32)
    total += jnp.dot(other_j[0], block[1 - x], preferred_element_type=F32)
    if has_sum:
        total += rest[0][0]
    rest[-1][0] = total


def add_gamma(place, mine, same_j, other_j, block, shape, before, fresh):
    n_j, cols, depth = block.shape
    half, rows = same_j.shape[0], same_j.shape[1]
    tile = depth // 2 if depth % 256 == 0 else depth

    def target(p, i, s):
        return (s[1] if mine else 1 - s[1]) * half + i, 0, p

    pair = pl.BlockSpec((1, rows, cols), lambda p, i, s: (i, 0, 0))
    out_spec = pl.BlockSpec((1, rows, tile), target)
    in_specs = [pair, pair, pl.BlockSpec((n_j, cols, tile), lambda p, i, s: (0, 0, p))]
    args = [place, same_j, other_j, block]
    aliases = {}
    if before is not None:
        in_specs.append(ANY if fresh else out_spec)
        args.append(before)
        aliases = {len(args) - 1: 0}
    out = jax.ShapeDtypeStruct(shape, F32)
    moved = jax.ShapeDtypeStruct((half, rows, depth), F32)
    return pl.pallas_call(
        functools.partial(gamma_kernel, not fresh),
        out_shape=out,
        grid_spec=pltpu.PrefetchScalarGridSpec(
            num_scalar_prefetch=1,
            grid=(depth // tile, half),
            in_specs=in_specs,
            out_specs=out_spec,
        ),
        input_output_aliases=aliases,
        compiler_params=PARAMS,
        cost_estimate=cost(2 * n_j * half * rows * cols * depth, moved, moved, block, same_j, other_j),
        name="add_gamma",
    )(*args)


def chain_device(b_occ_i, b_occ_j, eps_occ_i, eps_occ_j, eps_vir):
    n_i, rows, depth = b_occ_i.shape
    half = n_i // 2
    z, col = lax.axis_index("row"), lax.axis_index("col")
    x, core = col // 2, col % 2
    place = jnp.stack([x, core]).astype(jnp.int32)
    occ = lax.dynamic_slice_in_dim(eps_occ_i, core * half, half, 0) + eps_occ_j[x]

    def energies(block):
        return lax.dynamic_slice_in_dim(eps_vir, block * rows, rows, 0)

    vir_a = energies(z)[:, None]
    to_core = [(q, q ^ 1) for q in range(4)]
    to_chip = [(q, q ^ 2) for q in range(4)]

    def along(values, steps):
        return lax.ppermute(values, "row", steps)

    ends, middle = [(1, 0), (2, 3)], [(1, 2), (2, 1)]
    near = along(b_occ_j, [(k, k ^ 1) for k in range(4)])
    across = along(b_occ_j, middle)
    far_end = along(across, ends)
    far_mid = along(near, middle)
    far = jnp.where((z == 1) | (z == 2), far_mid, far_end)
    last = along(far_mid, ends)

    rounds = [
        (b_occ_j, 0, None),
        (near, 1, [(0, 1), (1, 0), (2, 3), (3, 2)]),
        (across, 3, middle),
        (far, 2, [(0, 2), (2, 0), (1, 3), (3, 1)]),
        (last, 3, [(0, 3), (3, 0)]),
    ]
    gamma = None
    for block, shift, swap in rounds:
        vir_b = energies(z ^ shift)[None, :]
        from_core = lax.ppermute(pairs_for_core(place, b_occ_i, block), "col", to_core)
        from_chip = lax.ppermute(pairs_for_chip(place, b_occ_i, block, from_core), "col", to_chip)
        held = own_amplitudes(place, occ, b_occ_i, block, from_core, from_chip, vir_a, vir_b)
        mirror = held if swap is None else along(held, swap)
        combined = combine_pairs(held, mirror)
        other_j = lax.ppermute(combined, "col", to_chip)
        core_same = lax.ppermute(combined, "col", to_core)
        core_other = lax.ppermute(other_j, "col", to_core)
        first = gamma is None
        gamma = add_gamma(place, True, combined, other_j, block, b_occ_i.shape, gamma, first)
        gamma = add_gamma(place, False, core_same, core_other, block, b_occ_i.shape, gamma, first)
    return gamma


def general_device(b_occ_i, b_occ_j, eps_occ_i, eps_occ_j, eps_vir):
    rows = b_occ_i.shape[1]
    own_energy = lax.dynamic_slice_in_dim(eps_vir, lax.axis_index("row") * rows, rows, 0)
    gathered = lax.all_gather(b_occ_j, "row", axis=1, tiled=True)
    partial_value = jnp.einsum("iap,jbp->jiab", b_occ_i, gathered, preferred_element_type=F32)
    totals = lax.psum(partial_value.astype(BF16), "col").astype(F32)
    denominator = (
        eps_occ_j[:, None, None, None]
        + eps_occ_i[None, :, None, None]
        - own_energy[None, None, :, None]
        - eps_vir[None, None, None, :]
    )
    held = (totals / denominator).astype(BF16)
    mirror = jnp.swapaxes(lax.all_to_all(held, "row", split_axis=3, concat_axis=2, tiled=True), 2, 3)
    combined = (2.0 * held.astype(F32) - mirror.astype(F32)).astype(BF16)
    return jnp.einsum("jiab,jbp->iap", combined, gathered, preferred_element_type=F32)


def solution(mesh):
    placed = (
        P("groups", "row", "col"),
        P("groups", "row", "col"),
        P("groups"),
        P("groups"),
        P("groups"),
    )
    chain = mesh.shape["row"] == 4 and mesh.shape["col"] == 4
    return jax.shard_map(
        chain_device if chain else general_device,
        mesh=mesh,
        in_specs=placed,
        out_specs=P("groups", "row", "col"),
        check_vma=False,
    )
```

```python
import functools

import jax
import jax.numpy as jnp
from jax import lax
from jax.experimental import pallas as pl
from jax.experimental.pallas import tpu as pltpu
from jax.sharding import PartitionSpec as P

F32 = jnp.float32
BF16 = jnp.bfloat16
ANY = pl.BlockSpec(memory_space=pl.ANY)
TOKEN = jax.ShapeDtypeStruct((8, 128), F32)
TILE = 256


def tile_of(size):
    return TILE if size % TILE == 0 else size


def call(kernel, name, token, place, grid, in_specs, args, out_specs, out, aliases=None):
    def body(*refs):
        n = len(place)
        kernel(*refs[:n], *refs[n + 1 : -1])

    shift = len(place) + 1
    return pl.pallas_call(
        body,
        out_shape=(*out, TOKEN),
        grid_spec=pltpu.PrefetchScalarGridSpec(
            num_scalar_prefetch=len(place),
            grid=grid,
            in_specs=[ANY] + in_specs,
            out_specs=(*out_specs, ANY),
        ),
        input_output_aliases={k + shift: v for k, v in (aliases or {}).items()},
        compiler_params=pltpu.CompilerParams(vmem_limit_bytes=60 * 2**20),
        cost_estimate=pl.CostEstimate(flops=0, bytes_accessed=1024, transcendentals=0),
        name=name,
    )(*place, token, *args)


def tie_kernel(place, held, out):
    del place, held, out


def tie(token, place, held):
    return call(tie_kernel, "tie", token, place, (1,), [ANY], [held], [ANY], [held_shape(held)], {0: 0})


def held_shape(a):
    return jax.ShapeDtypeStruct(a.shape, a.dtype)


def pairs_kernel(n_place, n_more, *refs):
    place, rest = refs[:n_place], refs[n_place:]
    b_i, block, rest = rest[0], rest[1], rest[2:]
    out = rest[-1]
    half, rows, depth = b_i.shape
    left = b_i[...].reshape(half * rows, depth)
    total = lax.dot_general(left, block[0], (((1,), (1,)), ((), ())), preferred_element_type=F32)
    for i in range(half):
        value = total[i * rows : (i + 1) * rows]
        if n_more > 0:
            value = value + rest[0][i].astype(F32)
        if n_more > 1:
            chip, vir_a, vir_b = rest[1:4]
            value = value + chip[i].astype(F32)
            value = value / ((place[1][i] - vir_a[...]) - vir_b[...])
        out[i] = value.astype(BF16)


def pairs(token, place, b_i, block, own_i, own_j, core=None, last=None):
    n_j, cols, depth = block.shape
    half, rows = b_i.shape[0] // 2, b_i.shape[1]
    tile = tile_of(cols)

    def j_of(s):
        return s[0] if own_j else 1 - s[0]

    every = pl.BlockSpec((half, rows, tile), lambda t, s, *_: (0, 0, t))
    in_specs = [
        pl.BlockSpec((half, rows, depth), lambda t, s, *_: (s[1] if own_i else 1 - s[1], 0, 0)),
        pl.BlockSpec((1, tile, depth), lambda t, s, *_: (j_of(s), t, 0)),
    ]
    args, n_more, name = [b_i, block], 0, "pairs_for_core"
    if core is not None:
        in_specs.append(every)
        args.append(core)
        n_more, name = 1, "pairs_for_chip"
    if last is not None:
        chip, occ, vir_a, vir_b = last
        place = place + (occ,)
        in_specs += [
            every,
            pl.BlockSpec((rows, 1), lambda t, s, *_: (0, 0)),
            pl.BlockSpec((1, tile), lambda t, s, *_: (0, t)),
        ]
        args += [chip, vir_a, vir_b]
        n_more, name = 2, "own_amplitudes"
    out = jax.ShapeDtypeStruct((half, rows, cols), BF16)
    kernel = functools.partial(pairs_kernel, len(place), n_more)
    return call(kernel, name, token, place, (cols // tile,), in_specs, args, [every], [out])


def combine_kernel(place, held, mirror, out):
    out[0] = (2.0 * held[0].astype(F32) - mirror[0].astype(F32).T).astype(BF16)


def combine_pairs(token, place, held, mirror):
    spec = pl.BlockSpec((1,) + held.shape[1:], lambda i, s: (i, 0, 0))
    return call(
        combine_kernel, "combine_pairs", token, place, held.shape[:1], [spec, spec], [held, mirror], [spec], [held_shape(held)]
    )


def gamma_kernel(n_blocks, has_sum, place, *refs):
    x = place[0]
    out = refs[-1]
    half, rows, tile = out.shape
    total = refs[-2][...].reshape(half * rows, tile) if has_sum else None
    for k in range(n_blocks):
        same_j, other_j, block = refs[3 * k : 3 * k + 3]
        for held, j in ((same_j, x), (other_j, 1 - x)):
            left = held[...].reshape(half * rows, held.shape[2])
            term = jnp.dot(left, block[j], preferred_element_type=F32)
            total = term if total is None else total + term
    out[...] = total.reshape(half, rows, tile)


def add_gamma(token, place, mine, terms, shape, before, fresh):
    half, rows, depth = shape[0] // 2, shape[1], shape[2]
    tile = tile_of(depth)
    out_spec = pl.BlockSpec((half, rows, tile), lambda p, s: (s[1] if mine else 1 - s[1], 0, p))
    in_specs, args = [], []
    for same_j, other_j, block in terms:
        held = [same_j, other_j]
        in_specs += [pl.BlockSpec(h.shape, lambda p, s: (0, 0, 0)) for h in held]
        in_specs.append(pl.BlockSpec(block.shape[:2] + (tile,), lambda p, s: (0, 0, p)))
        args += [*held, block]
    aliases = None
    if before is not None:
        aliases = {len(args): 0}
        in_specs.append(ANY if fresh else out_spec)
        args.append(before)
    kernel = functools.partial(gamma_kernel, len(terms), not fresh)
    return call(
        kernel, "add_gamma", token, place, (depth // tile,), in_specs, args, [out_spec], [jax.ShapeDtypeStruct(shape, F32)], aliases
    )


def chain_device(b_occ_i, b_occ_j, eps_occ_i, eps_occ_j, eps_vir):
    n_i, rows, depth = b_occ_i.shape
    half = n_i // 2
    z, col = lax.axis_index("row"), lax.axis_index("col")
    x, core = col // 2, col % 2
    place = (jnp.stack([x, core]).astype(jnp.int32),)
    occ = lax.dynamic_slice_in_dim(eps_occ_i, core * half, half, 0) + eps_occ_j[x]
    token = jnp.zeros(TOKEN.shape, F32)

    def energies(block):
        return lax.dynamic_slice_in_dim(eps_vir, block * rows, rows, 0)

    vir_a = energies(z)[:, None]

    def to_core(values):
        return lax.ppermute(values, "col", [(q, q ^ 1) for q in range(4)])

    def to_chip(values):
        return lax.ppermute(values, "col", [(q, q ^ 2) for q in range(4)])

    def along(values, steps):
        return lax.ppermute(values, "row", steps)

    ends, middle = [(1, 0), (2, 3)], [(1, 2), (2, 1)]
    pairs_1 = [(0, 1), (1, 0), (2, 3), (3, 2)]
    pairs_2 = [(0, 2), (2, 0), (1, 3), (3, 1)]
    pairs_3 = [(0, 3), (3, 0)]
    in_middle = (z == 1) | (z == 2)

    def send(block, own_j):
        nonlocal token
        out, token = pairs(token, place, b_occ_i, block, False, own_j)
        return to_core(out)

    def pass_on(block, core_sum):
        nonlocal token
        out, token = pairs(token, place, b_occ_i, block, True, False, core_sum)
        return to_chip(out)

    def own(block, core_sum, chip_sum, shift):
        nonlocal token
        vir_b = energies(z ^ shift)[None, :]
        out, token = pairs(token, place, b_occ_i, block, True, True, core_sum, (chip_sum, occ, vir_a, vir_b))
        return out

    def combine(held, mirror):
        nonlocal token
        out, token = combine_pairs(token, place, held, mirror)
        return out, to_chip(out), to_core(out)

    def forward(values):
        nonlocal token
        out, token = tie(token, place, values)
        return out

    def spread(other):
        other = forward(other)
        return other, to_core(other)

    gamma = None

    def add(mine, terms, fresh=False):
        nonlocal token, gamma
        gamma, token = add_gamma(token, place, mine, terms, b_occ_i.shape, gamma, fresh)

    near = along(b_occ_j, pairs_1)
    across = along(b_occ_j, middle)

    pass_0 = send(b_occ_j, False)
    keep_0 = send(b_occ_j, True)
    chip_0 = pass_on(b_occ_j, pass_0)
    held_0 = own(b_occ_j, keep_0, chip_0, 0)
    mine_0, other_0, same_0 = combine(held_0, held_0)

    near = forward(near)
    across = forward(across)
    far_mid = along(near, middle)
    far_end = along(across, ends)
    pass_1 = send(near, False)
    pass_12 = send(across, False)
    keep_1 = send(near, True)
    chip_1 = pass_on(near, pass_1)
    keep_12 = send(across, True)
    chip_12 = pass_on(across, pass_12)

    other_0, both_0 = spread(other_0)
    add(True, [(mine_0, other_0, b_occ_j)], True)
    add(False, [(same_0, both_0, b_occ_j)], True)

    held_1 = own(near, keep_1, chip_1, 1)
    mirror_1 = along(held_1, pairs_1)

    far_mid = forward(far_mid)
    last = along(far_mid, ends)
    far = jnp.where(in_middle, far_mid, far_end)
    pass_2 = send(far, False)
    keep_2 = send(far, True)
    chip_2 = pass_on(far, pass_2)

    held_12 = own(across, keep_12, chip_12, 3)
    mirror_12 = along(held_12, middle)

    mine_1, other_1, same_1 = combine(held_1, mirror_1)

    held_2 = own(far, keep_2, chip_2, 2)
    mirror_2 = along(held_2, pairs_2)

    mine_12, other_12, same_12 = combine(held_12, mirror_12)

    last = forward(last)
    pass_3 = send(last, False)
    keep_3 = send(last, True)
    chip_3 = pass_on(last, pass_3)

    other_1, both_1 = spread(other_1)
    other_12, both_12 = spread(other_12)
    add(True, [(mine_1, other_1, near), (mine_12, other_12, across)])
    add(False, [(same_1, both_1, near), (same_12, both_12, across)])

    mine_2, other_2, same_2 = combine(held_2, mirror_2)
    held_3 = own(last, keep_3, chip_3, 3)
    mirror_3 = along(held_3, pairs_3)

    other_2, both_2 = spread(other_2)
    add(True, [(mine_2, other_2, far)])
    add(False, [(same_2, both_2, far)])

    mine_3, other_3, same_3 = combine(held_3, mirror_3)
    other_3, both_3 = spread(other_3)
    add(True, [(mine_3, other_3, last)])
    add(False, [(same_3, both_3, last)])
    return gamma


def general_device(b_occ_i, b_occ_j, eps_occ_i, eps_occ_j, eps_vir):
    rows = b_occ_i.shape[1]
    own_energy = lax.dynamic_slice_in_dim(eps_vir, lax.axis_index("row") * rows, rows, 0)
    gathered = lax.all_gather(b_occ_j, "row", axis=1, tiled=True)
    partial_value = jnp.einsum("iap,jbp->jiab", b_occ_i, gathered, preferred_element_type=F32)
    totals = lax.psum(partial_value.astype(BF16), "col").astype(F32)
    denominator = (
        eps_occ_j[:, None, None, None]
        + eps_occ_i[None, :, None, None]
        - own_energy[None, None, :, None]
        - eps_vir[None, None, None, :]
    )
    held = (totals / denominator).astype(BF16)
    mirror = jnp.swapaxes(lax.all_to_all(held, "row", split_axis=3, concat_axis=2, tiled=True), 2, 3)
    combined = (2.0 * held.astype(F32) - mirror.astype(F32)).astype(BF16)
    return jnp.einsum("jiab,jbp->iap", combined, gathered, preferred_element_type=F32)


def solution(mesh):
    placed = (
        P("groups", "row", "col"),
        P("groups", "row", "col"),
        P("groups"),
        P("groups"),
        P("groups"),
    )
    chain = mesh.shape["row"] == 4 and mesh.shape["col"] == 4
    return jax.shard_map(
        chain_device if chain else general_device,
        mesh=mesh,
        in_specs=placed,
        out_specs=P("groups", "row", "col"),
        check_vma=False,
    )
```

```python
import functools

import jax
import jax.numpy as jnp
from jax import lax
from jax.experimental import pallas as pl
from jax.experimental.pallas import tpu as pltpu
from jax.sharding import PartitionSpec as P

F32 = jnp.float32
BF16 = jnp.bfloat16
ANY = pl.BlockSpec(memory_space=pl.ANY)
TOKEN = jax.ShapeDtypeStruct((8, 128), F32)
TILE = 256


def tile_of(size):
    return TILE if size % TILE == 0 else size


def call(kernel, name, token, place, grid, in_specs, args, out_specs, out, aliases=None):
    def body(*refs):
        n = len(place)
        kernel(*refs[:n], *refs[n + 1 : -1])

    shift = len(place) + 1
    return pl.pallas_call(
        body,
        out_shape=(*out, TOKEN),
        grid_spec=pltpu.PrefetchScalarGridSpec(
            num_scalar_prefetch=len(place),
            grid=grid,
            in_specs=[ANY] + in_specs,
            out_specs=(*out_specs, ANY),
        ),
        input_output_aliases={k + shift: v for k, v in (aliases or {}).items()},
        compiler_params=pltpu.CompilerParams(vmem_limit_bytes=40 * 2**20),
        cost_estimate=pl.CostEstimate(flops=0, bytes_accessed=1024, transcendentals=0),
        name=name,
    )(*place, token, *args)


def tie_kernel(place, *refs):
    del place, refs


def tie(token, place, *held):
    n = len(held)
    shapes = [held_shape(h) for h in held]
    return call(tie_kernel, "tie", token, place, (1,), [ANY] * n, held, [ANY] * n, shapes, {k: k for k in range(n)})


def held_shape(a):
    return jax.ShapeDtypeStruct(a.shape, a.dtype)


def takes_part(place, part):
    return place[3 if part == "middle" else 4] == 1


def only(place, part, out):
    def run(body):
        if part is None:
            body()
            return
        pl.when(takes_part(place, part))(body)

        @pl.when(jnp.logical_not(takes_part(place, part)))
        def _():
            out[...] = jnp.zeros_like(out)

    return run


def pairs_kernel(n_place, has_last, part, *refs):
    place, (b_i, b_i_core, block, block_core, *rest) = refs[:n_place], refs[n_place:]
    out = rest[-1]
    across = (((1,), (1,)), ((), ()))

    @only(place[0], part, out)
    def _():
        value = lax.dot_general(b_i[0], block[0], across, preferred_element_type=F32)
        value += lax.dot_general(b_i_core[0], block_core[0], across, preferred_element_type=F32)
        if has_last:
            chip, vir_a, vir_b = rest[:3]
            value = value + chip[0].astype(F32)
            value = value / ((place[1][pl.program_id(0)] - vir_a[...]) - vir_b[...])
        out[0] = value.astype(BF16)


def pairs(token, place, b_i, block, own_j, part, last=None):
    (mine, core_part), (block, block_core) = b_i, block
    n_j, cols, depth = block.shape
    half, rows = core_part.shape[:2]

    def j_of(s):
        return s[0] if own_j else 1 - s[0]

    one = pl.BlockSpec((1, rows, cols), lambda i, s, *_: (i, 0, 0))
    block_spec = pl.BlockSpec((1, cols, depth), lambda i, s, *_: (j_of(s), 0, 0))
    in_specs = [
        pl.BlockSpec((1, rows, depth), lambda i, s, *_: (s[1] * half + i, 0, 0)),
        pl.BlockSpec((1, rows, depth), lambda i, s, *_: (i, 0, 0)),
        block_spec,
        block_spec,
    ]
    args, name = [mine, core_part, block, block_core], "pairs_for_chip"
    if last is not None:
        chip, occ, vir_a, vir_b = last
        place = place + (occ,)
        in_specs += [
            one,
            pl.BlockSpec((rows, 1), lambda i, s, *_: (0, 0)),
            pl.BlockSpec((1, cols), lambda i, s, *_: (0, 0)),
        ]
        args += [chip, vir_a, vir_b]
        name = "own_amplitudes"
    out = jax.ShapeDtypeStruct((half, rows, cols), BF16)
    kernel = functools.partial(pairs_kernel, len(place), last is not None, part)
    return call(kernel, name, token, place, (half,), in_specs, args, [one], [out])


def combine_kernel(part, place, held, mirror, out):
    @only(place, part, out)
    def _():
        out[0] = (2.0 * held[0].astype(F32) - mirror[0].astype(F32).T).astype(BF16)


def combine_pairs(token, place, held, mirror, part):
    spec = pl.BlockSpec((1,) + held.shape[1:], lambda i, s: (i, 0, 0))
    kernel = functools.partial(combine_kernel, part)
    return call(kernel, "combine_pairs", token, place, held.shape[:1], [spec, spec], [held, mirror], [spec], [held_shape(held)])


def gamma_kernel(n_blocks, n_out, has_sum, place, *refs):
    x = place[0]
    outs = refs[len(refs) - n_out :]
    befores = refs[len(refs) - 2 * n_out : len(refs) - n_out]
    half, rows, tile = outs[0].shape
    step = 2 + n_out
    for k in range(n_out):
        total = befores[k][...].reshape(half * rows, tile) if has_sum else None
        for n in range(n_blocks):
            same_j, other_j = refs[step * n : step * n + 2]
            block = refs[step * n + 2 + k]
            for held, j in ((same_j, x), (other_j, 1 - x)):
                left = held[...].reshape(half * rows, held.shape[2])
                term = jnp.dot(left, block[j], preferred_element_type=F32)
                total = term if total is None else total + term
        outs[k][...] = total.reshape(half, rows, tile)


def gamma_operands(terms, tile):
    in_specs, args = [], []
    for *held, blocks in terms:
        in_specs += [pl.BlockSpec(h.shape, lambda p, s: (0, 0, 0), pipeline_mode=pl.Buffered(1)) for h in held]
        in_specs += [pl.BlockSpec(b.shape[:2] + (tile,), lambda p, s: (0, 0, p)) for b in blocks]
        args += [*held, *blocks]
    return in_specs, args


def chip_gamma(token, place, terms, before):
    half, rows = terms[0][0].shape[:2]
    depth = terms[0][2][0].shape[2]
    tile = tile_of(depth)
    in_specs, args = gamma_operands(terms, tile)
    spec = pl.BlockSpec((half, rows, tile), lambda p, s: (0, 0, p))
    aliases = None
    if before is not None:
        aliases = {len(args): 0, len(args) + 1: 1}
        in_specs += [spec, spec]
        args += before
    out = [jax.ShapeDtypeStruct((half, rows, depth), F32)] * 2
    kernel = functools.partial(gamma_kernel, len(terms), 2, before is not None)
    *out, token = call(kernel, "chip_gamma", token, place, (depth // tile,), in_specs, args, [spec, spec], out, aliases)
    return out, token


def last_gamma(token, place, mine, terms, before, shape, result):
    half, rows, depth = shape[0] // 2, shape[1], shape[2]
    tile = tile_of(depth)
    in_specs, args = gamma_operands(terms, tile)
    spec = pl.BlockSpec((half, rows, tile), lambda p, s: (0, 0, p))
    aliases, out_spec, out = None, spec, held_shape(before)
    if mine is None:
        aliases = {len(args): 0}
    else:
        out_spec = pl.BlockSpec((half, rows, tile), lambda p, s: (s[1] if mine else 1 - s[1], 0, p))
        out = jax.ShapeDtypeStruct(shape, F32)
    if result is not None:
        aliases = {len(args): 0}
        in_specs.append(ANY)
        args.append(result)
    in_specs.append(spec)
    args.append(before)
    kernel = functools.partial(gamma_kernel, len(terms), 1, True)
    return call(kernel, "last_gamma", token, place, (depth // tile,), in_specs, args, [out_spec], [out], aliases)


def chain_device(b_occ_i, b_occ_j, eps_occ_i, eps_occ_j, eps_vir):
    n_i, rows, depth = b_occ_i.shape
    half = n_i // 2
    z, col = lax.axis_index("row"), lax.axis_index("col")
    x, core = col // 2, col % 2
    in_middle = (z == 1) | (z == 2)
    place = (jnp.stack([x, core, z, in_middle, ~in_middle]).astype(jnp.int32),)
    occ = lax.dynamic_slice_in_dim(eps_occ_i, core * half, half, 0) + eps_occ_j[x]
    token = jnp.zeros(TOKEN.shape, F32)

    def energies(block):
        return lax.dynamic_slice_in_dim(eps_vir, block * rows, rows, 0)

    vir_a = energies(z)[:, None]

    def to_col(values, flip, part):
        rows_in = {None: range(4), "middle": (1, 2), "ends": (0, 3)}[part]
        steps = [(4 * r + q, 4 * r + (q ^ flip)) for r in rows_in for q in range(4)]
        return lax.ppermute(values, ("row", "col"), steps)

    def to_core(values, part=None):
        return to_col(values, 1, part)

    def to_chip(values, part=None):
        return to_col(values, 2, part)

    def along(values, steps):
        return lax.ppermute(values, "row", steps)

    ends, middle = [(1, 0), (2, 3)], [(1, 2), (2, 1)]
    pairs_1 = [(0, 1), (1, 0), (2, 3), (3, 2)]
    pairs_2 = [(0, 2), (2, 0), (1, 3), (3, 1)]
    pairs_3 = [(0, 3), (3, 0)]
    b_i = b_occ_i, to_core(lax.dynamic_slice_in_dim(b_occ_i, (1 - core) * half, half, 0))

    def pass_on(block, part=None):
        nonlocal token
        out, token = pairs(token, place, b_i, block, False, part)
        return to_chip(out, part)

    def own(block, chip_sum, shift, part=None):
        nonlocal token
        vir_b = energies(z ^ shift)[None, :]
        out, token = pairs(token, place, b_i, block, True, part, (chip_sum, occ, vir_a, vir_b))
        return out

    def combine(held, mirror, part=None):
        nonlocal token
        out, token = combine_pairs(token, place, held, mirror, part)
        return out, to_chip(out, part)

    def forward(*values):
        nonlocal token
        *out, token = tie(token, place, *values)
        return out

    gamma = None

    def add(*terms):
        nonlocal token, gamma
        gamma, token = chip_gamma(token, place, terms, gamma)

    def both(values, part=None):
        return values, to_core(values, part)

    near = along(b_occ_j, pairs_1)
    across = along(b_occ_j, middle)
    here = both(b_occ_j)

    chip_0 = pass_on(here)
    held_0 = own(here, chip_0, 0)
    mine_0, other_0 = combine(held_0, held_0)

    near, across = forward(near, across)
    far_mid = along(near, middle)
    far_end = along(across, ends)
    near = both(near)
    across = both(across, "middle")
    chip_1 = pass_on(near)
    chip_12 = pass_on(across, "middle")

    add((mine_0, other_0, here))

    held_1 = own(near, chip_1, 1)
    mirror_1 = along(held_1, pairs_1)

    (far_mid,) = forward(far_mid)
    last = along(far_mid, ends)
    far = both(jnp.where(in_middle, far_mid, far_end))
    chip_2 = pass_on(far)

    held_12 = own(across, chip_12, 3, "middle")
    mirror_12 = along(held_12, middle)

    mine_1, other_1 = combine(held_1, mirror_1)
    held_2 = own(far, chip_2, 2)
    mirror_2 = along(held_2, pairs_2)
    mine_12, other_12 = combine(held_12, mirror_12, "middle")

    add((mine_1, other_1, near))
    gamma, rest = gamma[0], to_core(gamma[1])
    shape = b_occ_i.shape

    (last,) = forward(last)
    last = both(last, "ends")
    chip_3 = pass_on(last, "ends")

    same_12 = to_core(mine_12, "middle")
    (other_12,) = forward(other_12)
    both_12 = to_core(other_12, "middle")

    mine_2, other_2 = combine(held_2, mirror_2)
    same_2 = to_core(mine_2)
    held_3 = own(last, chip_3, 3, "ends")
    mirror_3 = along(held_3, pairs_3)

    (other_2,) = forward(other_2)
    both_2 = to_core(other_2)
    terms = [(mine_12, other_12, across[:1]), (mine_2, other_2, far[:1])]
    gamma, token = last_gamma(token, place, None, terms, gamma, shape, None)

    mine_3, other_3 = combine(held_3, mirror_3, "ends")
    same_3 = to_core(mine_3, "ends")
    terms = [(same_12, both_12, across[:1]), (same_2, both_2, far[:1])]
    rest, token = last_gamma(token, place, None, terms, rest, shape, None)

    (other_3,) = forward(other_3)
    both_3 = to_core(other_3, "ends")
    result, token = last_gamma(token, place, True, [(mine_3, other_3, last[:1])], gamma, shape, None)
    result, token = last_gamma(token, place, False, [(same_3, both_3, last[:1])], rest, shape, result)
    return result


def general_device(b_occ_i, b_occ_j, eps_occ_i, eps_occ_j, eps_vir):
    rows = b_occ_i.shape[1]
    own_energy = lax.dynamic_slice_in_dim(eps_vir, lax.axis_index("row") * rows, rows, 0)
    gathered = lax.all_gather(b_occ_j, "row", axis=1, tiled=True)
    partial_value = jnp.einsum("iap,jbp->jiab", b_occ_i, gathered, preferred_element_type=F32)
    totals = lax.psum(partial_value.astype(BF16), "col").astype(F32)
    denominator = (
        eps_occ_j[:, None, None, None]
        + eps_occ_i[None, :, None, None]
        - own_energy[None, None, :, None]
        - eps_vir[None, None, None, :]
    )
    held = (totals / denominator).astype(BF16)
    mirror = jnp.swapaxes(lax.all_to_all(held, "row", split_axis=3, concat_axis=2, tiled=True), 2, 3)
    combined = (2.0 * held.astype(F32) - mirror.astype(F32)).astype(BF16)
    return jnp.einsum("jiab,jbp->iap", combined, gathered, preferred_element_type=F32)


def solution(mesh):
    placed = (
        P("groups", "row", "col"),
        P("groups", "row", "col"),
        P("groups"),
        P("groups"),
        P("groups"),
    )
    chain = mesh.shape["row"] == 4 and mesh.shape["col"] == 4
    return jax.shard_map(
        chain_device if chain else general_device,
        mesh=mesh,
        in_specs=placed,
        out_specs=P("groups", "row", "col"),
        check_vma=False,
    )
```

```python
import functools

import jax
import jax.numpy as jnp
from jax import lax
from jax.experimental import pallas as pl
from jax.experimental.pallas import tpu as pltpu
from jax.sharding import PartitionSpec as P

F32 = jnp.float32
BF16 = jnp.bfloat16
ANY = pl.BlockSpec(memory_space=pl.ANY)
TOKEN = jax.ShapeDtypeStruct((8, 128), F32)
TILE = 256


def tile_of(size):
    return TILE if size % TILE == 0 else size


def call(kernel, name, token, place, grid, in_specs, args, out_specs, out, aliases=None):
    def body(*refs):
        n = len(place)
        kernel(*refs[:n], *refs[n + 1 : -1])

    shift = len(place) + 1
    return pl.pallas_call(
        body,
        out_shape=(*out, TOKEN),
        grid_spec=pltpu.PrefetchScalarGridSpec(
            num_scalar_prefetch=len(place),
            grid=grid,
            in_specs=[ANY] + in_specs,
            out_specs=(*out_specs, ANY),
        ),
        input_output_aliases={k + shift: v for k, v in (aliases or {}).items()},
        compiler_params=pltpu.CompilerParams(vmem_limit_bytes=56 * 2**20),
        cost_estimate=pl.CostEstimate(flops=0, bytes_accessed=1024, transcendentals=0),
        name=name,
    )(*place, token, *args)


def tie_kernel(place, *refs):
    del place, refs


def tie(token, place, *held):
    n = len(held)
    shapes = [held_shape(h) for h in held]
    return call(tie_kernel, "tie", token, place, (1,), [ANY] * n, held, [ANY] * n, shapes, {k: k for k in range(n)})


def held_shape(a):
    return jax.ShapeDtypeStruct(a.shape, a.dtype)


def takes_part(place, part):
    return place[3 if part == "middle" else 4] == 1


def only(place, part, out):
    def run(body):
        if part is None:
            body()
            return
        pl.when(takes_part(place, part))(body)

        @pl.when(jnp.logical_not(takes_part(place, part)))
        def _():
            out[...] = jnp.zeros_like(out)

    return run


def whole_block(pieces, j):
    return jnp.concatenate([p[j] for p in pieces], axis=0) if len(pieces) > 1 else pieces[0][j]


def pairs_kernel(n_place, n_pieces, has_last, part, first, *refs):
    place, (b_i, b_i_core, block, *rest) = refs[:n_place], refs[n_place:]
    pieces, rest, out = rest[:n_pieces], rest[n_pieces:], rest[-1]
    across = (((1,), (1,)), ((), ()))

    @only(place[0], part, out)
    def _():
        value = lax.dot_general(b_i[0], block[0], across, preferred_element_type=F32)
        value += lax.dot_general(b_i_core[0], whole_block(pieces, 0), across, preferred_element_type=F32)
        if has_last:
            chip, vir_a, vir_b = rest[:3]
            value = value + chip[0].astype(F32)
            value = value / ((place[1][first + pl.program_id(0)] - vir_a[...]) - vir_b[...])
        out[0] = value.astype(BF16)


def pairs(token, place, b_i, block, own_j, part, which=None, last=None):
    (mine, core_part), (block, pieces) = b_i, block
    n_j, cols, depth = block.shape
    half, rows = core_part.shape[:2]
    first, count = (0, half) if which is None else (which, 1)

    def j_of(s):
        return s[0] if own_j else 1 - s[0]

    one = pl.BlockSpec((1, rows, cols), lambda i, s, *_: (i, 0, 0))
    block_specs = [pl.BlockSpec((1,) + p.shape[1:], lambda i, s, *_: (j_of(s), 0, 0)) for p in (block, *pieces)]
    in_specs = [
        pl.BlockSpec((1, rows, depth), lambda i, s, *_: (s[1] * half + first + i, 0, 0)),
        pl.BlockSpec((1, rows, depth), lambda i, s, *_: (first + i, 0, 0)),
    ] + block_specs
    args, name = [mine, core_part, block, *pieces], "pairs_for_chip"
    if last is not None:
        chip, occ, vir_a, vir_b = last
        place = place + (occ,)
        in_specs += [
            one,
            pl.BlockSpec((rows, 1), lambda i, s, *_: (0, 0)),
            pl.BlockSpec((1, cols), lambda i, s, *_: (0, 0)),
        ]
        args += [chip, vir_a, vir_b]
        name = "own_amplitudes"
    out = jax.ShapeDtypeStruct((count, rows, cols), BF16)
    kernel = functools.partial(pairs_kernel, len(place), len(pieces), last is not None, part, first)
    return call(kernel, name, token, place, (count,), in_specs, args, [one], [out])


def combine_kernel(part, place, held, mirror, *outs):
    for i, out in enumerate(outs):

        @pl.when((pl.program_id(0) == i) | (len(outs) == 1))
        def _():
            @only(place, part, out)
            def _():
                out[0] = (2.0 * held[0].astype(F32) - mirror[0].astype(F32).T).astype(BF16)


def combine_pairs(token, place, held, mirror, part, split):
    count, rows, cols = held.shape
    spec = pl.BlockSpec((1, rows, cols), lambda i, s: (i, 0, 0))
    out_specs, out = [spec], [held_shape(held)]
    if split:
        out_specs = [pl.BlockSpec((1, rows, cols), lambda i, s: (0, 0, 0))] * count
        out = [jax.ShapeDtypeStruct((1, rows, cols), BF16)] * count
    kernel = functools.partial(combine_kernel, part)
    *out, token = call(kernel, "combine_pairs", token, place, (count,), [spec, spec], [held, mirror], out_specs, out)
    return (out if split else out[0]), token


def gamma_kernel(terms, has_sum, place, *refs):
    x = place[0]
    refs, outs = list(refs[:-2]), refs[-2:]
    count, rows, tile = outs[0].shape
    held = []
    for own_pieces, core_pieces, part in terms:
        pairs, refs = refs[:2], refs[2:]
        blocks, refs = (refs[:own_pieces], refs[own_pieces : own_pieces + core_pieces]), refs[own_pieces + core_pieces :]
        held.append((pairs, blocks, part))

    def share(k, pairs, blocks):
        total = None
        for pair, j in zip(pairs, (x, 1 - x)):
            left = pair[...].reshape(count * rows, pair.shape[2])
            term = jnp.dot(left, whole_block(blocks[k], j), preferred_element_type=F32)
            total = term if total is None else total + term
        return total.reshape(count, rows, tile)

    for k, out in enumerate(outs):
        total = refs[k][...] if has_sum else None
        for pairs, blocks, part in held:
            if part is None:
                total = share(k, pairs, blocks) if total is None else total + share(k, pairs, blocks)
        if all(part is None for *_, part in held):
            out[...] = total.astype(out.dtype)
            continue
        out[...] = total
        for pairs, blocks, part in held:
            if part is not None:

                @pl.when(takes_part(place, part))
                def _():
                    out[...] += share(k, pairs, blocks)


def gamma_operands(terms, which, tile):
    in_specs, args, counts = [], [], []
    for same_j, other_j, (block, pieces), part in terms:
        for h in (same_j, other_j):
            if which is None or h.shape[0] == 1:
                in_specs.append(pl.BlockSpec(h.shape, lambda p, s: (0, 0, 0)))
            else:
                in_specs.append(pl.BlockSpec((1,) + h.shape[1:], lambda p, s: (which, 0, 0)))
        in_specs += [pl.BlockSpec(b.shape[:2] + (tile,), lambda p, s: (0, 0, p)) for b in (block, *pieces)]
        args += [same_j, other_j, block, *pieces]
        counts.append((1, len(pieces), part))
    return in_specs, args, counts


def chip_gamma(token, place, terms, before=None):
    half, rows = terms[0][0].shape[:2]
    depth = terms[0][2][0].shape[2]
    tile = tile_of(depth)
    in_specs, args, counts = gamma_operands(terms, None, tile)
    spec = pl.BlockSpec((half, rows, tile), lambda p, s: (0, 0, p))
    aliases = None
    if before is not None:
        aliases = {len(args): 0, len(args) + 1: 1}
        in_specs += [spec, spec]
        args += before
    out = [jax.ShapeDtypeStruct((half, rows, depth), F32)] * 2
    kernel = functools.partial(gamma_kernel, counts, before is not None)
    *out, token = call(kernel, "chip_gamma", token, place, (depth // tile,), in_specs, args, [spec, spec], out, aliases)
    return out, token


def last_gamma(token, place, which, terms, before, shape, result):
    half, rows, depth = before[0].shape
    tile = tile_of(depth)
    in_specs, args, counts = gamma_operands(terms, which, tile)
    spec = pl.BlockSpec((1, rows, tile), lambda p, s: (which, 0, p))
    in_specs += [spec, spec]
    args += before
    aliases, drop = None, 0
    if result is not None:
        aliases, drop = {len(args): 0}, 1
        in_specs.append(ANY)
        args.append(result)

    def kernel(place, *refs):
        n = len(refs) - 2
        gamma_kernel(counts, True, place, *refs[: n - drop], *refs[n:])

    out_specs = [
        pl.BlockSpec((1, rows, tile), lambda p, s: (s[1] * half + which, 0, p)),
        pl.BlockSpec((1, rows, tile), lambda p, s: (0, 0, p)),
    ]
    out = [jax.ShapeDtypeStruct(shape, F32), jax.ShapeDtypeStruct((1, rows, depth), BF16)]
    return call(kernel, "last_gamma", token, place, (depth // tile,), in_specs, args, out_specs, out, aliases)


def place_kernel(place, received, result, out):
    del place, result
    out[...] = received[...].astype(F32)


def place_gamma(token, place, which, received, result):
    half = result.shape[0] // 2
    _, rows, depth = received.shape
    tile = rows // 2
    return call(
        place_kernel,
        "place_gamma",
        token,
        place,
        (2,),
        [pl.BlockSpec((1, tile, depth), lambda p, s: (0, p, 0)), ANY],
        [received, result],
        [pl.BlockSpec((1, tile, depth), lambda p, s: ((1 - s[1]) * half + which, p, 0))],
        [held_shape(result)],
        {1: 0},
    )


def chain_device(b_occ_i, b_occ_j, eps_occ_i, eps_occ_j, eps_vir):
    n_i, rows, depth = b_occ_i.shape
    half = n_i // 2
    z, col = lax.axis_index("row"), lax.axis_index("col")
    x, core = col // 2, col % 2
    in_middle = (z == 1) | (z == 2)
    place = (jnp.stack([x, core, z, in_middle, ~in_middle]).astype(jnp.int32),)
    occ = lax.dynamic_slice_in_dim(eps_occ_i, core * half, half, 0) + eps_occ_j[x]
    token = jnp.zeros(TOKEN.shape, F32)

    def energies(block):
        return lax.dynamic_slice_in_dim(eps_vir, block * rows, rows, 0)

    vir_a = energies(z)[:, None]

    def to_col(values, flip, part):
        rows_in = {None: range(4), "middle": (1, 2), "ends": (0, 3)}[part]
        steps = [(4 * r + q, 4 * r + (q ^ flip)) for r in rows_in for q in range(4)]
        return lax.ppermute(values, ("row", "col"), steps)

    def to_core(values, part=None):
        return to_col(values, 1, part)

    def to_chip(values, part=None):
        return to_col(values, 2, part)

    def along(values, steps):
        return lax.ppermute(values, "row", steps)

    ends, middle = [(1, 0), (2, 3)], [(1, 2), (2, 1)]
    pairs_1 = [(0, 1), (1, 0), (2, 3), (3, 2)]
    pairs_2 = [(0, 2), (2, 0), (1, 3), (3, 1)]
    pairs_3 = [(0, 3), (3, 0)]
    b_i = b_occ_i, to_core(lax.dynamic_slice_in_dim(b_occ_i, (1 - core) * half, half, 0))

    def pass_on(block, part=None, which=None):
        nonlocal token
        out, token = pairs(token, place, b_i, block, False, part, which)
        return to_chip(out, part)

    def own(block, chip_sum, shift, part=None, which=None):
        nonlocal token
        vir_b = energies(z ^ shift)[None, :]
        out, token = pairs(token, place, b_i, block, True, part, which, (chip_sum, occ, vir_a, vir_b))
        return out

    def combine(held, mirror, part=None, split=False):
        nonlocal token
        out, token = combine_pairs(token, place, held, mirror, part, split)
        return out

    def forward(*values):
        nonlocal token
        *out, token = tie(token, place, *values)
        return out

    def both(values, part=None, n_pieces=1):
        return values, [to_core(p, part) for p in jnp.split(values, n_pieces, axis=1)]

    shape = b_occ_i.shape
    near = along(b_occ_j, pairs_1)
    across = along(b_occ_j, middle)
    here = both(b_occ_j)

    chip_0 = pass_on(here)
    held_0 = own(here, chip_0, 0)
    mine_0 = combine(held_0, held_0)

    near, across = forward(near, across)
    far_mid = along(near, middle)
    far_end = along(across, ends)
    near = both(near)
    across = both(across, "middle")
    chip_1 = pass_on(near)
    chip_12 = pass_on(across, "middle")

    held_1 = own(near, chip_1, 1)
    mirror_1 = along(held_1, pairs_1)
    (mine_0,) = forward(mine_0)
    other_0 = to_chip(mine_0)

    far_mid, far_end = forward(far_mid, far_end)
    last = along(far_mid, ends)
    far = both(jnp.where(in_middle, far_mid, far_end))
    chip_2 = pass_on(far)

    held_12 = own(across, chip_12, 3, "middle")
    mirror_12 = along(held_12, middle)
    gamma, token = chip_gamma(token, place, [(mine_0, other_0, here, None)])

    held_2 = own(far, chip_2, 2)
    mirror_2 = along(held_2, pairs_2)
    mine_1 = combine(held_1, mirror_1)
    other_1 = to_chip(mine_1)
    mine_12 = combine(held_12, mirror_12, "middle")
    other_12 = to_chip(mine_12, "middle")
    other_1, other_12 = forward(other_1, other_12)

    (last,) = forward(last)
    last = both(last, "ends", 4)
    chip_3 = [pass_on(last, "ends", i) for i in range(half)]

    terms = [(mine_1, other_1, near, None), (mine_12, other_12, across, "middle")]
    gamma, token = chip_gamma(token, place, terms, gamma)

    held_3 = [own(last, chip_3[i], 3, "ends", i) for i in range(half)]
    mirror_3 = [along(h, pairs_3) for h in held_3]

    mine_2 = combine(held_2, mirror_2, split=True)
    other_2 = [to_chip(m) for m in mine_2]
    mine_3 = [combine(h, m, "ends") for h, m in zip(held_3, mirror_3)]
    other_3 = [to_chip(m, "ends") for m in mine_3]

    result, received = None, []
    for i in range(half):
        terms = [(mine_2[i], other_2[i], far, None), (mine_3[i], other_3[i], last, None)]
        result, theirs, token = last_gamma(token, place, i, terms, gamma, shape, result)
        received.append(to_core(theirs))
    for i in range(half):
        result, token = place_gamma(token, place, i, received[i], result)
    return result


def general_device(b_occ_i, b_occ_j, eps_occ_i, eps_occ_j, eps_vir):
    rows = b_occ_i.shape[1]
    own_energy = lax.dynamic_slice_in_dim(eps_vir, lax.axis_index("row") * rows, rows, 0)
    gathered = lax.all_gather(b_occ_j, "row", axis=1, tiled=True)
    partial_value = jnp.einsum("iap,jbp->jiab", b_occ_i, gathered, preferred_element_type=F32)
    totals = lax.psum(partial_value.astype(BF16), "col").astype(F32)
    denominator = (
        eps_occ_j[:, None, None, None]
        + eps_occ_i[None, :, None, None]
        - own_energy[None, None, :, None]
        - eps_vir[None, None, None, :]
    )
    held = (totals / denominator).astype(BF16)
    mirror = jnp.swapaxes(lax.all_to_all(held, "row", split_axis=3, concat_axis=2, tiled=True), 2, 3)
    combined = (2.0 * held.astype(F32) - mirror.astype(F32)).astype(BF16)
    return jnp.einsum("jiab,jbp->iap", combined, gathered, preferred_element_type=F32)


def solution(mesh):
    placed = (
        P("groups", "row", "col"),
        P("groups", "row", "col"),
        P("groups"),
        P("groups"),
        P("groups"),
    )
    chain = mesh.shape["row"] == 4 and mesh.shape["col"] == 4
    return jax.shard_map(
        chain_device if chain else general_device,
        mesh=mesh,
        in_specs=placed,
        out_specs=P("groups", "row", "col"),
        check_vma=False,
    )
```

```python
import functools

import jax
import jax.numpy as jnp
from jax import lax
from jax.experimental import pallas as pl
from jax.experimental.pallas import tpu as pltpu
from jax.sharding import PartitionSpec as P

F32 = jnp.float32
BF16 = jnp.bfloat16
ANY = pl.BlockSpec(memory_space=pl.ANY)
TOKEN = jax.ShapeDtypeStruct((8, 128), F32)
TILE = 256


def tile_of(size):
    return TILE if size % TILE == 0 else size


def call(kernel, name, token, place, grid, in_specs, args, out_specs, out, aliases=None, mib=8):
    def body(*refs):
        n = len(place)
        kernel(*refs[:n], *refs[n + 1 : -1])

    shift = len(place) + 1
    return pl.pallas_call(
        body,
        out_shape=(*out, TOKEN),
        grid_spec=pltpu.PrefetchScalarGridSpec(
            num_scalar_prefetch=len(place),
            grid=grid,
            in_specs=[ANY] + in_specs,
            out_specs=(*out_specs, ANY),
        ),
        input_output_aliases={k + shift: v for k, v in (aliases or {}).items()},
        compiler_params=pltpu.CompilerParams(vmem_limit_bytes=mib * 2**20),
        cost_estimate=pl.CostEstimate(flops=0, bytes_accessed=1024, transcendentals=0),
        name=name,
    )(*place, token, *args)


def tie_kernel(place, *refs):
    del place, refs


def tie(token, place, *held):
    n = len(held)
    shapes = [held_shape(h) for h in held]
    return call(tie_kernel, "tie", token, place, (1,), [ANY] * n, held, [ANY] * n, shapes, {k: k for k in range(n)})


def held_shape(a):
    return jax.ShapeDtypeStruct(a.shape, a.dtype)


def whole_block(pieces, j):
    return jnp.concatenate([p[j] for p in pieces], axis=0) if len(pieces) > 1 else pieces[0][j]


def pairs_kernel(n_place, n_pieces, has_last, first, *refs):
    place, (b_i, b_i_core, block, *rest) = refs[:n_place], refs[n_place:]
    pieces, rest, out = rest[:n_pieces], rest[n_pieces:], rest[-1]
    across = (((1,), (1,)), ((), ()))
    value = lax.dot_general(b_i[0], block[0], across, preferred_element_type=F32)
    value += lax.dot_general(b_i_core[0], whole_block(pieces, 0), across, preferred_element_type=F32)
    if has_last:
        chip, vir_a, vir_b = rest[:3]
        value = value + chip[0].astype(F32)
        value = value / ((place[1][first + pl.program_id(0)] - vir_a[...]) - vir_b[...])
    out[0] = value.astype(BF16)


def pairs(token, place, b_i, block, own_j, which=None, last=None):
    (mine, core_part), (block, passed, kept) = b_i, block
    pieces = kept if own_j else passed
    cols, depth = block.shape[1:]
    half, rows = core_part.shape[:2]
    first, count = (0, half) if which is None else (which, 1)

    def j_of(s):
        return s[0] if own_j else 1 - s[0]

    one = pl.BlockSpec((1, rows, cols), lambda i, s, *_: (i, 0, 0))
    in_specs = [
        pl.BlockSpec((1, rows, depth), lambda i, s, *_: (s[1] * half + first + i, 0, 0)),
        pl.BlockSpec((1, rows, depth), lambda i, s, *_: (first + i, 0, 0)),
        pl.BlockSpec((1, cols, depth), lambda i, s, *_: (j_of(s), 0, 0)),
    ]
    for p in pieces:
        one_j = p.shape[0] == 1
        in_specs.append(pl.BlockSpec((1,) + p.shape[1:], lambda i, s, *_, one_j=one_j: (0 if one_j else j_of(s), 0, 0)))
    args, name = [mine, core_part, block, *pieces], "pairs_for_chip"
    if last is not None:
        chip, occ, vir_a, vir_b = last
        place = place + (occ,)
        in_specs += [
            one,
            pl.BlockSpec((rows, 1), lambda i, s, *_: (0, 0)),
            pl.BlockSpec((1, cols), lambda i, s, *_: (0, 0)),
        ]
        args += [chip, vir_a, vir_b]
        name = "own_amplitudes"
    out = jax.ShapeDtypeStruct((count, rows, cols), BF16)
    kernel = functools.partial(pairs_kernel, len(place), len(pieces), last is not None, first)
    return call(kernel, name, token, place, (count,), in_specs, args, [one], [out], mib=24)


def combine_kernel(place, held, mirror, *outs):
    for i, out in enumerate(outs):

        @pl.when((pl.program_id(0) == i) | (len(outs) == 1))
        def _():
            out[0] = (2.0 * held[0].astype(F32) - mirror[0].astype(F32).T).astype(BF16)


def combine_pairs(token, place, held, mirror, split):
    count, rows, cols = held.shape
    spec = pl.BlockSpec((1, rows, cols), lambda i, s: (i, 0, 0))
    out_specs, out = [spec], [held_shape(held)]
    if split:
        out_specs = [pl.BlockSpec((1, rows, cols), lambda i, s: (0, 0, 0))] * count
        out = [jax.ShapeDtypeStruct((1, rows, cols), BF16)] * count
    *out, token = call(combine_kernel, "combine_pairs", token, place, (count,), [spec, spec], [held, mirror], out_specs, out, mib=12)
    return (out if split else out[0]), token


def gamma_kernel(terms, has_sum, place, *refs):
    x = place[0]
    refs, outs = list(refs[:-2]), refs[-2:]
    count, rows, tile = outs[0].shape
    held = []
    for n_passed, n_kept in terms:
        same_j, other_j, block = refs[:3]
        passed, kept = refs[3 : 3 + n_passed], refs[3 + n_passed : 3 + n_passed + n_kept]
        refs = refs[3 + n_passed + n_kept :]
        core_j = (0, 0) if n_kept else (x, 1 - x)
        held.append((same_j, (lambda block=block: block[x], lambda kept=kept or passed, j=core_j[0]: whole_block(kept, j))))
        held.append((other_j, (lambda block=block: block[1 - x], lambda passed=passed, j=core_j[1]: whole_block(passed, j))))
    for k, out in enumerate(outs):
        total = refs[k][...].reshape(count * rows, tile) if has_sum else None
        for pair, blocks in held:
            left = pair[...].reshape(count * rows, pair.shape[2])
            term = jnp.dot(left, blocks[k](), preferred_element_type=F32)
            total = term if total is None else total + term
        out[...] = total.reshape(count, rows, tile).astype(out.dtype)


def gamma_operands(terms, which, tile):
    in_specs, args, counts = [], [], []
    for same_j, other_j, (block, passed, kept) in terms:
        for h in (same_j, other_j):
            if which is None or h.shape[0] == 1:
                in_specs.append(pl.BlockSpec(h.shape, lambda p, s: (0, 0, 0), pipeline_mode=pl.Buffered(1)))
            else:
                in_specs.append(pl.BlockSpec((1,) + h.shape[1:], lambda p, s: (which, 0, 0)))
        kept = [] if kept is passed else kept
        blocks = [block, *passed, *kept]
        in_specs += [pl.BlockSpec(b.shape[:2] + (tile,), lambda p, s: (0, 0, p)) for b in blocks]
        args += [same_j, other_j, *blocks]
        counts.append((len(passed), len(kept)))
    return in_specs, args, counts


def chip_gamma(token, place, terms, before=None):
    half, rows = terms[0][0].shape[:2]
    depth = terms[0][2][0].shape[2]
    tile = tile_of(depth)
    in_specs, args, counts = gamma_operands(terms, None, tile)
    spec = pl.BlockSpec((half, rows, tile), lambda p, s: (0, 0, p))
    aliases = None
    if before is not None:
        aliases = {len(args): 0, len(args) + 1: 1}
        in_specs += [spec, spec]
        args += before
    out = [jax.ShapeDtypeStruct((half, rows, depth), F32)] * 2
    kernel = functools.partial(gamma_kernel, counts, before is not None)
    *out, token = call(kernel, "chip_gamma", token, place, (depth // tile,), in_specs, args, [spec, spec], out, aliases, mib=36)
    return out, token


def last_gamma(token, place, which, terms, before, shape, result):
    half, rows, depth = before[0].shape
    tile = tile_of(depth)
    in_specs, args, counts = gamma_operands(terms, which, tile)
    spec = pl.BlockSpec((1, rows, tile), lambda p, s: (which, 0, p))
    in_specs += [spec, spec]
    args += before
    aliases, drop = None, 0
    if result is not None:
        aliases, drop = {len(args): 0}, 1
        in_specs.append(ANY)
        args.append(result)

    def kernel(place, *refs):
        n = len(refs) - 2
        gamma_kernel(counts, True, place, *refs[: n - drop], *refs[n:])

    out_specs = [
        pl.BlockSpec((1, rows, tile), lambda p, s: (s[1] * half + which, 0, p)),
        pl.BlockSpec((1, rows, tile), lambda p, s: (0, 0, p)),
    ]
    out = [jax.ShapeDtypeStruct(shape, F32), jax.ShapeDtypeStruct((1, rows, depth), BF16)]
    return call(kernel, "last_gamma", token, place, (depth // tile,), in_specs, args, out_specs, out, aliases, mib=24)


def place_kernel(place, received, result, out):
    del place, result
    out[...] = received[...].astype(F32)


def place_gamma(token, place, which, received, result):
    half = result.shape[0] // 2
    _, rows, depth = received.shape
    tile = rows // 2
    return call(
        place_kernel,
        "place_gamma",
        token,
        place,
        (2,),
        [pl.BlockSpec((1, tile, depth), lambda p, s: (0, p, 0)), ANY],
        [received, result],
        [pl.BlockSpec((1, tile, depth), lambda p, s: ((1 - s[1]) * half + which, p, 0))],
        [held_shape(result)],
        {1: 0},
    )


def chain_device(b_occ_i, b_occ_j, eps_occ_i, eps_occ_j, eps_vir):
    n_i, rows, depth = b_occ_i.shape
    half = n_i // 2
    z, col = lax.axis_index("row"), lax.axis_index("col")
    x, core = col // 2, col % 2
    in_middle = (z == 1) | (z == 2)
    place = (jnp.stack([x, core]).astype(jnp.int32),)
    occ = lax.dynamic_slice_in_dim(eps_occ_i, core * half, half, 0) + eps_occ_j[x]
    token = jnp.zeros(TOKEN.shape, F32)
    shape = b_occ_i.shape

    def energies(block):
        return lax.dynamic_slice_in_dim(eps_vir, block * rows, rows, 0)

    vir_a = energies(z)[:, None]

    def to_core(values):
        return lax.ppermute(values, "col", [(q, q ^ 1) for q in range(4)])

    def to_chip(values):
        return lax.ppermute(values, "col", [(q, q ^ 2) for q in range(4)])

    def along(values, steps):
        return lax.ppermute(values, "row", steps)

    def swapped(values, distance):
        return along(values, [(k, k ^ distance) for k in range(4)])

    ends, middle = [(1, 0), (2, 3)], [(1, 2), (2, 1)]
    b_i = b_occ_i, to_core(lax.dynamic_slice_in_dim(b_occ_i, (1 - core) * half, half, 0))

    def pass_on(block, which=None):
        nonlocal token
        out, token = pairs(token, place, b_i, block, False, which)
        return to_chip(out)

    def own(block, chip_sum, distance, which=None):
        nonlocal token
        vir_b = energies(z ^ distance)[None, :]
        out, token = pairs(token, place, b_i, block, True, which, (chip_sum, occ, vir_a, vir_b))
        return out

    def combine(held, mirror, split=False):
        nonlocal token
        out, token = combine_pairs(token, place, held, mirror, split)
        return out

    def forward(*values):
        nonlocal token
        *out, token = tie(token, place, *values)
        return out

    def both(values):
        pieces = [to_core(values)]
        return values, pieces, pieces

    def both_in_pieces(values, n_pieces=2):
        def part(j):
            one = lax.dynamic_slice_in_dim(values, j, 1, 0)
            return [to_core(p) for p in jnp.split(one, n_pieces, axis=1)]

        return values, part(1 - x), part(x)

    near = swapped(b_occ_j, 1)
    across = along(b_occ_j, middle)
    here = both(b_occ_j)

    chip_0 = pass_on(here)
    held_0 = own(here, chip_0, 0)
    mine_0 = combine(held_0, held_0)
    other_0 = to_chip(mine_0)

    near, across = forward(near, across)
    far_mid = along(near, middle)
    far_end = along(across, ends)
    near = both(near)
    chip_1 = pass_on(near)
    gamma, token = chip_gamma(token, place, [(mine_0, other_0, here)])

    far_mid, far_end = forward(far_mid, far_end)
    last = along(far_mid, ends)
    far = both_in_pieces(jnp.where(in_middle, far_mid, far_end))
    held_1 = own(near, chip_1, 1)
    mirror_1 = swapped(held_1, 1)
    chip_2 = pass_on(far)

    held_2 = own(far, chip_2, 2)
    mirror_2 = swapped(held_2, 2)
    mine_1 = combine(held_1, mirror_1)
    other_1 = to_chip(mine_1)

    (last,) = forward(last)
    last = both_in_pieces(jnp.where(in_middle, across, last))
    chip_3 = [pass_on(last, 0)]
    last = last[:2] + (forward(*last[2]),)
    chip_3 += [pass_on(last, i) for i in range(1, half)]
    gamma, token = chip_gamma(token, place, [(mine_1, other_1, near)], gamma)
    mine_2 = combine(held_2, mirror_2, split=True)
    other_2 = [to_chip(m) for m in mine_2]
    held_3 = [own(last, chip_3[i], 3, i) for i in range(half)]
    mirror_3 = [swapped(h, 3) for h in held_3]
    mine_3 = [combine(h, m) for h, m in zip(held_3, mirror_3)]
    other_3 = [to_chip(m) for m in mine_3]

    result, received = None, []
    for i in range(half):
        terms = [(mine_2[i], other_2[i], far), (mine_3[i], other_3[i], last)]
        result, theirs, token = last_gamma(token, place, i, terms, gamma, shape, result)
        received.append(to_core(theirs))
    for i in range(half):
        result, token = place_gamma(token, place, i, received[i], result)
    return result


def general_device(b_occ_i, b_occ_j, eps_occ_i, eps_occ_j, eps_vir):
    rows = b_occ_i.shape[1]
    own_energy = lax.dynamic_slice_in_dim(eps_vir, lax.axis_index("row") * rows, rows, 0)
    gathered = lax.all_gather(b_occ_j, "row", axis=1, tiled=True)
    partial_value = jnp.einsum("iap,jbp->jiab", b_occ_i, gathered, preferred_element_type=F32)
    totals = lax.psum(partial_value.astype(BF16), "col").astype(F32)
    denominator = (
        eps_occ_j[:, None, None, None]
        + eps_occ_i[None, :, None, None]
        - own_energy[None, None, :, None]
        - eps_vir[None, None, None, :]
    )
    held = (totals / denominator).astype(BF16)
    mirror = jnp.swapaxes(lax.all_to_all(held, "row", split_axis=3, concat_axis=2, tiled=True), 2, 3)
    combined = (2.0 * held.astype(F32) - mirror.astype(F32)).astype(BF16)
    return jnp.einsum("jiab,jbp->iap", combined, gathered, preferred_element_type=F32)


def solution(mesh):
    placed = (
        P("groups", "row", "col"),
        P("groups", "row", "col"),
        P("groups"),
        P("groups"),
        P("groups"),
    )
    chain = mesh.shape["row"] == 4 and mesh.shape["col"] == 4
    return jax.shard_map(
        chain_device if chain else general_device,
        mesh=mesh,
        in_specs=placed,
        out_specs=P("groups", "row", "col"),
        check_vma=False,
    )
```

```python
import functools

import jax
import jax.numpy as jnp
from jax import lax
from jax.experimental import pallas as pl
from jax.experimental.pallas import tpu as pltpu
from jax.sharding import PartitionSpec as P

F32 = jnp.float32
BF16 = jnp.bfloat16
ANY = pl.BlockSpec(memory_space=pl.ANY)
TOKEN = jax.ShapeDtypeStruct((8, 128), F32)
TILE = 256


def in_hbm(a):
    return pltpu.with_memory_space_constraint(a, pltpu.HBM)


def tile_of(size):
    return TILE if size % TILE == 0 else size


def call(kernel, name, token, place, grid, in_specs, args, out_specs, out, aliases=None, mib=8):
    def body(*refs):
        n = len(place)
        kernel(*refs[:n], *refs[n + 1 : -1])

    shift = len(place) + 1
    return pl.pallas_call(
        body,
        out_shape=(*out, TOKEN),
        grid_spec=pltpu.PrefetchScalarGridSpec(
            num_scalar_prefetch=len(place),
            grid=grid,
            in_specs=[ANY] + in_specs,
            out_specs=(*out_specs, ANY),
        ),
        input_output_aliases={k + shift: v for k, v in (aliases or {}).items()},
        compiler_params=pltpu.CompilerParams(vmem_limit_bytes=mib * 2**20),
        cost_estimate=pl.CostEstimate(flops=0, bytes_accessed=1024, transcendentals=0),
        name=name,
    )(*place, token, *args)


def tie_kernel(place, *refs):
    del place, refs


def tie(token, place, *held):
    n = len(held)
    shapes = [held_shape(h) for h in held]
    return call(tie_kernel, "tie", token, place, (1,), [ANY] * n, held, [ANY] * n, shapes, {k: k for k in range(n)})


def held_shape(a):
    return jax.ShapeDtypeStruct(a.shape, a.dtype)


def whole_block(pieces, j):
    return jnp.concatenate([p[j] for p in pieces], axis=0) if len(pieces) > 1 else pieces[0][j]


def pairs_kernel(n_place, n_pieces, has_last, first, *refs):
    place, (b_i, b_i_core, block, *rest) = refs[:n_place], refs[n_place:]
    pieces, rest, out = rest[:n_pieces], rest[n_pieces:], rest[-1]
    across = (((1,), (1,)), ((), ()))
    value = lax.dot_general(b_i[0], block[0], across, preferred_element_type=F32)
    value += lax.dot_general(b_i_core[0], whole_block(pieces, 0), across, preferred_element_type=F32)
    if has_last:
        chip, vir_a, vir_b = rest[:3]
        value = value + chip[0].astype(F32)
        value = value / ((place[1][first + pl.program_id(0)] - vir_a[...]) - vir_b[...])
    out[0] = value.astype(BF16)


def pairs(token, place, b_i, block, own_j, which=None, last=None):
    (mine, core_part), (block, passed, kept) = b_i, block
    pieces = kept if own_j else passed
    cols, depth = block.shape[1:]
    half, rows = core_part.shape[0] // 2, core_part.shape[1]
    first, count = (0, half) if which is None else (which, 1)

    def j_of(s):
        return s[0] if own_j else 1 - s[0]

    one = pl.BlockSpec((1, rows, cols), lambda i, s, *_: (i, 0, 0))
    in_specs = [
        pl.BlockSpec((1, rows, depth), lambda i, s, *_: (s[1] * half + first + i, 0, 0)),
        pl.BlockSpec((1, rows, depth), lambda i, s, *_: (s[1] * half + first + i, 0, 0)),
        pl.BlockSpec((1, cols, depth), lambda i, s, *_: (j_of(s), 0, 0)),
    ]
    for p in pieces:
        one_j = p.shape[0] == 1
        in_specs.append(pl.BlockSpec((1,) + p.shape[1:], lambda i, s, *_, one_j=one_j: (0 if one_j else j_of(s), 0, 0)))
    args, name = [mine, core_part, block, *pieces], "pairs_for_chip"
    if last is not None:
        chip, occ, vir_a, vir_b = last
        place = place + (occ,)
        in_specs += [
            one,
            pl.BlockSpec((rows, 1), lambda i, s, *_: (0, 0)),
            pl.BlockSpec((1, cols), lambda i, s, *_: (0, 0)),
        ]
        args += [chip, vir_a, vir_b]
        name = "own_amplitudes"
    out = jax.ShapeDtypeStruct((count, rows, cols), BF16)
    kernel = functools.partial(pairs_kernel, len(place), len(pieces), last is not None, first)
    return call(kernel, name, token, place, (count,), in_specs, args, [one], [out], mib=24)


def combine_kernel(place, held, mirror, *outs):
    for i, out in enumerate(outs):

        @pl.when((pl.program_id(0) == i) | (len(outs) == 1))
        def _():
            out[0] = (2.0 * held[0].astype(F32) - mirror[0].astype(F32).T).astype(BF16)


def combine_pairs(token, place, held, mirror, split):
    count, rows, cols = held.shape
    spec = pl.BlockSpec((1, rows, cols), lambda i, s: (i, 0, 0))
    out_specs, out = [spec], [held_shape(held)]
    if split:
        out_specs = [pl.BlockSpec((1, rows, cols), lambda i, s: (0, 0, 0))] * count
        out = [jax.ShapeDtypeStruct((1, rows, cols), BF16)] * count
    *out, token = call(combine_kernel, "combine_pairs", token, place, (count,), [spec, spec], [held, mirror], out_specs, out, mib=12)
    return (out if split else out[0]), token


def gamma_kernel(terms, has_sum, place, *refs):
    x = place[0]
    refs, outs = list(refs[:-2]), refs[-2:]
    count, rows, tile = outs[0].shape
    held = []
    for n_passed, n_kept in terms:
        same_j, other_j, block = refs[:3]
        passed, kept = refs[3 : 3 + n_passed], refs[3 + n_passed : 3 + n_passed + n_kept]
        refs = refs[3 + n_passed + n_kept :]
        core_j = (0, 0) if n_kept else (x, 1 - x)
        held.append((same_j, (lambda block=block: block[x], lambda kept=kept or passed, j=core_j[0]: whole_block(kept, j))))
        held.append((other_j, (lambda block=block: block[1 - x], lambda passed=passed, j=core_j[1]: whole_block(passed, j))))
    for k, out in enumerate(outs):
        total = refs[k][...].reshape(count * rows, tile) if has_sum else None
        for pair, blocks in held:
            left = pair[...].reshape(count * rows, pair.shape[2])
            term = jnp.dot(left, blocks[k](), preferred_element_type=F32)
            total = term if total is None else total + term
        out[...] = total.reshape(count, rows, tile).astype(out.dtype)


def gamma_operands(terms, which, tile):
    in_specs, args, counts = [], [], []
    for same_j, other_j, (block, passed, kept) in terms:
        for h in (same_j, other_j):
            if which is None or h.shape[0] == 1:
                in_specs.append(pl.BlockSpec(h.shape, lambda p, s: (0, 0, 0), pipeline_mode=pl.Buffered(1)))
            else:
                in_specs.append(pl.BlockSpec((1,) + h.shape[1:], lambda p, s: (which, 0, 0)))
        kept = [] if kept is passed else kept
        blocks = [block, *passed, *kept]
        in_specs += [pl.BlockSpec(b.shape[:2] + (tile,), lambda p, s: (0, 0, p)) for b in blocks]
        args += [same_j, other_j, *blocks]
        counts.append((len(passed), len(kept)))
    return in_specs, args, counts


def chip_gamma(token, place, terms, before=None):
    half, rows = terms[0][0].shape[:2]
    depth = terms[0][2][0].shape[2]
    tile = tile_of(depth)
    in_specs, args, counts = gamma_operands(terms, None, tile)
    spec = pl.BlockSpec((half, rows, tile), lambda p, s: (0, 0, p))
    aliases = None
    if before is not None:
        aliases = {len(args): 0, len(args) + 1: 1}
        in_specs += [spec, spec]
        args += before
    out = [jax.ShapeDtypeStruct((half, rows, depth), F32)] * 2
    kernel = functools.partial(gamma_kernel, counts, before is not None)
    *out, token = call(kernel, "chip_gamma", token, place, (depth // tile,), in_specs, args, [spec, spec], out, aliases, mib=36)
    return out, token


def last_gamma(token, place, which, terms, before, shape, result):
    half, rows, depth = before[0].shape
    tile = tile_of(depth)
    in_specs, args, counts = gamma_operands(terms, which, tile)
    spec = pl.BlockSpec((1, rows, tile), lambda p, s: (which, 0, p))
    in_specs += [spec, spec]
    args += before
    aliases, drop = None, 0
    if result is not None:
        aliases, drop = {len(args): 0}, 1
        in_specs.append(ANY)
        args.append(result)

    def kernel(place, *refs):
        n = len(refs) - 2
        gamma_kernel(counts, True, place, *refs[: n - drop], *refs[n:])

    out_specs = [
        pl.BlockSpec((1, rows, tile), lambda p, s: (s[1] * half + which, 0, p)),
        pl.BlockSpec((1, rows, tile), lambda p, s: (0, 0, p)),
    ]
    out = [jax.ShapeDtypeStruct(shape, F32), jax.ShapeDtypeStruct((1, rows, depth), BF16)]
    return call(kernel, "last_gamma", token, place, (depth // tile,), in_specs, args, out_specs, out, aliases, mib=24)


def place_kernel(place, received, result, out):
    del place, result
    out[...] = received[...].astype(F32)


def place_gamma(token, place, which, received, result):
    half = result.shape[0] // 2
    _, rows, depth = received.shape
    tile = rows // 2
    return call(
        place_kernel,
        "place_gamma",
        token,
        place,
        (2,),
        [pl.BlockSpec((1, tile, depth), lambda p, s: (0, p, 0)), ANY],
        [received, result],
        [pl.BlockSpec((1, tile, depth), lambda p, s: ((1 - s[1]) * half + which, p, 0))],
        [held_shape(result)],
        {1: 0},
    )


def chain_device(b_occ_i, b_occ_j, eps_occ_i, eps_occ_j, eps_vir):
    n_i, rows, depth = b_occ_i.shape
    half = n_i // 2
    z, col = lax.axis_index("row"), lax.axis_index("col")
    x, core = col // 2, col % 2
    in_middle = (z == 1) | (z == 2)
    place = (jnp.stack([x, core]).astype(jnp.int32),)
    occ = lax.dynamic_slice_in_dim(eps_occ_i, core * half, half, 0) + eps_occ_j[x]
    token = jnp.zeros(TOKEN.shape, F32)
    shape = b_occ_i.shape

    def energies(block):
        return lax.dynamic_slice_in_dim(eps_vir, block * rows, rows, 0)

    vir_a = energies(z)[:, None]

    def to_core(values):
        return lax.ppermute(values, "col", [(q, q ^ 1) for q in range(4)])

    def to_chip(values):
        return lax.ppermute(values, "col", [(q, q ^ 2) for q in range(4)])

    def along(values, steps):
        return lax.ppermute(values, "row", steps)

    def swapped(values, distance):
        return along(values, [(k, k ^ distance) for k in range(4)])

    ends, middle = [(1, 0), (2, 3)], [(1, 2), (2, 1)]
    b_i = in_hbm(b_occ_i), in_hbm(to_core(b_occ_i))

    def pass_on(block, which=None):
        nonlocal token
        out, token = pairs(token, place, b_i, block, False, which)
        return to_chip(out)

    def own(block, chip_sum, distance, which=None):
        nonlocal token
        vir_b = energies(z ^ distance)[None, :]
        out, token = pairs(token, place, b_i, block, True, which, (chip_sum, occ, vir_a, vir_b))
        return out

    def combine(held, mirror, split=False):
        nonlocal token
        out, token = combine_pairs(token, place, held, mirror, split)
        return out

    def forward(*values):
        nonlocal token
        *out, token = tie(token, place, *values)
        return out

    def both(values):
        pieces = [to_core(values)]
        return values, pieces, pieces

    def in_pieces(values, own_j, n_pieces=2):
        one = lax.dynamic_slice_in_dim(values, x if own_j else 1 - x, 1, 0)
        return [to_core(p) for p in jnp.split(one, n_pieces, axis=1)]

    near = swapped(b_occ_j, 1)
    across = along(b_occ_j, middle)
    here = both(b_occ_j)

    chip_0 = pass_on(here)
    held_0 = own(here, chip_0, 0)

    near, across = forward(near, across)
    far_mid = along(near, middle)
    far_end = along(across, ends)
    near = both(near)
    mine_0 = combine(held_0, held_0)
    chip_1 = pass_on(near)

    held_1 = own(near, chip_1, 1)
    mirror_1 = swapped(held_1, 1)
    far_mid, far_end = forward(far_mid, far_end)
    last = along(far_mid, ends)
    far = jnp.where(in_middle, far_mid, far_end)
    far = far, in_pieces(far, False), in_pieces(far, True)
    chip_2 = pass_on(far)

    held_2 = own(far, chip_2, 2)
    mirror_2 = swapped(held_2, 2)
    (mine_0,) = forward(mine_0)
    other_0 = to_chip(mine_0)
    mine_1 = combine(held_1, mirror_1)
    other_1 = to_chip(mine_1)

    (last,) = forward(last)
    last = jnp.where(in_middle, across, last)
    passed = in_pieces(last, False)
    chip_3 = [pass_on((last, passed, None), 0)]
    mine_2 = combine(held_2, mirror_2, split=True)
    other_2 = [to_chip(m) for m in mine_2]
    (last,) = forward(last)
    last = last, passed, in_pieces(last, True)
    chip_3.append(pass_on(last, 1))
    other_0, other_1 = forward(other_0, other_1)
    chip_3 += [pass_on(last, i) for i in range(2, half)]
    held_3 = [own(last, chip_3[i], 3, i) for i in range(half)]
    mirror_3 = [swapped(h, 3) for h in held_3]
    gamma, token = chip_gamma(token, place, [(mine_0, other_0, here), (mine_1, other_1, near)])
    mine_3 = [combine(h, m) for h, m in zip(held_3, mirror_3)]
    other_3 = [to_chip(m) for m in mine_3]

    result, received = None, []
    for i in range(half):
        terms = [(mine_2[i], other_2[i], far), (mine_3[i], other_3[i], last)]
        result, theirs, token = last_gamma(token, place, i, terms, gamma, shape, result)
        received.append(to_core(theirs))
    for i in range(half):
        result, token = place_gamma(token, place, i, received[i], result)
    return result


def general_device(b_occ_i, b_occ_j, eps_occ_i, eps_occ_j, eps_vir):
    rows = b_occ_i.shape[1]
    own_energy = lax.dynamic_slice_in_dim(eps_vir, lax.axis_index("row") * rows, rows, 0)
    gathered = lax.all_gather(b_occ_j, "row", axis=1, tiled=True)
    partial_value = jnp.einsum("iap,jbp->jiab", b_occ_i, gathered, preferred_element_type=F32)
    totals = lax.psum(partial_value.astype(BF16), "col").astype(F32)
    denominator = (
        eps_occ_j[:, None, None, None]
        + eps_occ_i[None, :, None, None]
        - own_energy[None, None, :, None]
        - eps_vir[None, None, None, :]
    )
    held = (totals / denominator).astype(BF16)
    mirror = jnp.swapaxes(lax.all_to_all(held, "row", split_axis=3, concat_axis=2, tiled=True), 2, 3)
    combined = (2.0 * held.astype(F32) - mirror.astype(F32)).astype(BF16)
    return jnp.einsum("jiab,jbp->iap", combined, gathered, preferred_element_type=F32)


def solution(mesh):
    placed = (
        P("groups", "row", "col"),
        P("groups", "row", "col"),
        P("groups"),
        P("groups"),
        P("groups"),
    )
    chain = mesh.shape["row"] == 4 and mesh.shape["col"] == 4
    return jax.shard_map(
        chain_device if chain else general_device,
        mesh=mesh,
        in_specs=placed,
        out_specs=P("groups", "row", "col"),
        check_vma=False,
    )
```

```python
import functools

import jax
import jax.numpy as jnp
from jax import lax
from jax.experimental import pallas as pl
from jax.experimental.pallas import tpu as pltpu
from jax.sharding import PartitionSpec as P

F32 = jnp.float32
BF16 = jnp.bfloat16
ANY = pl.BlockSpec(memory_space=pl.ANY)
TOKEN = jax.ShapeDtypeStruct((8, 128), F32)
TILE = 256


def in_hbm(a):
    return pltpu.with_memory_space_constraint(a, pltpu.HBM)


def tile_of(size):
    return TILE if size % TILE == 0 else size


def call(kernel, name, token, place, grid, in_specs, args, out_specs, out, aliases=None, mib=8):
    def body(*refs):
        n = len(place)
        kernel(*refs[:n], *refs[n + 1 : -1])

    shift = len(place) + 1
    return pl.pallas_call(
        body,
        out_shape=(*out, TOKEN),
        grid_spec=pltpu.PrefetchScalarGridSpec(
            num_scalar_prefetch=len(place),
            grid=grid,
            in_specs=[ANY] + in_specs,
            out_specs=(*out_specs, ANY),
        ),
        input_output_aliases={k + shift: v for k, v in (aliases or {}).items()},
        compiler_params=pltpu.CompilerParams(vmem_limit_bytes=mib * 2**20),
        cost_estimate=pl.CostEstimate(flops=0, bytes_accessed=1024, transcendentals=0),
        name=name,
    )(*place, token, *args)


def tie_kernel(place, *refs):
    del place, refs


def tie(token, place, *held):
    n = len(held)
    shapes = [held_shape(h) for h in held]
    return call(tie_kernel, "tie", token, place, (1,), [ANY] * n, held, [ANY] * n, shapes, {k: k for k in range(n)})


def held_shape(a):
    return jax.ShapeDtypeStruct(a.shape, a.dtype)


def whole_block(pieces, j):
    return jnp.concatenate([p[j] for p in pieces], axis=0) if len(pieces) > 1 else pieces[0][j]


def pairs_kernel(n_place, n_pieces, has_last, first, *refs):
    place, (b_i, b_i_core, block, *rest) = refs[:n_place], refs[n_place:]
    pieces, rest, out = rest[:n_pieces], rest[n_pieces:], rest[-1]
    across = (((1,), (1,)), ((), ()))
    value = lax.dot_general(b_i[0], block[0], across, preferred_element_type=F32)
    value += lax.dot_general(b_i_core[0], whole_block(pieces, 0), across, preferred_element_type=F32)
    if has_last:
        chip, vir_a, vir_b = rest[:3]
        value = value + chip[0].astype(F32)
        value = value / ((place[1][first + pl.program_id(0)] - vir_a[...]) - vir_b[...])
    out[0] = value.astype(BF16)


def pairs(token, place, b_i, block, own_j, which=None, last=None):
    (mine, core_part), (block, passed, kept) = b_i, block
    pieces = kept if own_j else passed
    cols, depth = block.shape[1:]
    half, rows = core_part.shape[0] // 2, core_part.shape[1]
    first, count = (0, half) if which is None else (which, 1)

    def j_of(s):
        return s[0] if own_j else 1 - s[0]

    one = pl.BlockSpec((1, rows, cols), lambda i, s, *_: (i, 0, 0))
    in_specs = [
        pl.BlockSpec((1, rows, depth), lambda i, s, *_: (s[1] * half + first + i, 0, 0)),
        pl.BlockSpec((1, rows, depth), lambda i, s, *_: (s[1] * half + first + i, 0, 0)),
        pl.BlockSpec((1, cols, depth), lambda i, s, *_: (j_of(s), 0, 0)),
    ]
    for p in pieces:
        one_j = p.shape[0] == 1
        in_specs.append(pl.BlockSpec((1,) + p.shape[1:], lambda i, s, *_, one_j=one_j: (0 if one_j else j_of(s), 0, 0)))
    args, name = [mine, core_part, block, *pieces], "pairs_for_chip"
    if last is not None:
        chip, occ, vir_a, vir_b = last
        place = place + (occ,)
        in_specs += [
            one,
            pl.BlockSpec((rows, 1), lambda i, s, *_: (0, 0)),
            pl.BlockSpec((1, cols), lambda i, s, *_: (0, 0)),
        ]
        args += [chip, vir_a, vir_b]
        name = "own_amplitudes"
    out = jax.ShapeDtypeStruct((count, rows, cols), BF16)
    kernel = functools.partial(pairs_kernel, len(place), len(pieces), last is not None, first)
    return call(kernel, name, token, place, (count,), in_specs, args, [one], [out], mib=24)


def combine_kernel(place, held, mirror, *outs):
    for i, out in enumerate(outs):

        @pl.when((pl.program_id(0) == i) | (len(outs) == 1))
        def _():
            out[0] = (2.0 * held[0].astype(F32) - mirror[0].astype(F32).T).astype(BF16)


def combine_pairs(token, place, held, mirror, split):
    count, rows, cols = held.shape
    spec = pl.BlockSpec((1, rows, cols), lambda i, s: (i, 0, 0))
    out_specs, out = [spec], [held_shape(held)]
    if split:
        out_specs = [pl.BlockSpec((1, rows, cols), lambda i, s: (0, 0, 0))] * count
        out = [jax.ShapeDtypeStruct((1, rows, cols), BF16)] * count
    *out, token = call(combine_kernel, "combine_pairs", token, place, (count,), [spec, spec], [held, mirror], out_specs, out, mib=12)
    return (out if split else out[0]), token


def gamma_kernel(terms, has_sum, place, *refs):
    x = place[0]
    refs, outs = list(refs[:-2]), refs[-2:]
    count, rows, tile = outs[0].shape
    held = []
    for n_passed, n_kept in terms:
        same_j, other_j, block = refs[:3]
        passed, kept = refs[3 : 3 + n_passed], refs[3 + n_passed : 3 + n_passed + n_kept]
        refs = refs[3 + n_passed + n_kept :]
        core_j = (0, 0) if n_kept else (x, 1 - x)
        held.append((same_j, (lambda block=block: block[x], lambda kept=kept or passed, j=core_j[0]: whole_block(kept, j))))
        held.append((other_j, (lambda block=block: block[1 - x], lambda passed=passed, j=core_j[1]: whole_block(passed, j))))
    for k, out in enumerate(outs):
        total = refs[k][...].reshape(count * rows, tile) if has_sum else None
        for pair, blocks in held:
            left = pair[...].reshape(count * rows, pair.shape[2])
            term = jnp.dot(left, blocks[k](), preferred_element_type=F32)
            total = term if total is None else total + term
        out[...] = total.reshape(count, rows, tile).astype(out.dtype)


def gamma_operands(terms, which, tile):
    in_specs, args, counts = [], [], []
    for same_j, other_j, (block, passed, kept) in terms:
        for h in (same_j, other_j):
            if which is None or h.shape[0] == 1:
                in_specs.append(pl.BlockSpec(h.shape, lambda p, s: (0, 0, 0), pipeline_mode=pl.Buffered(1)))
            else:
                in_specs.append(pl.BlockSpec((1,) + h.shape[1:], lambda p, s: (which, 0, 0)))
        kept = [] if kept is passed else kept
        blocks = [block, *passed, *kept]
        in_specs += [pl.BlockSpec(b.shape[:2] + (tile,), lambda p, s: (0, 0, p)) for b in blocks]
        args += [same_j, other_j, *blocks]
        counts.append((len(passed), len(kept)))
    return in_specs, args, counts


def chip_gamma(token, place, terms, before=None):
    half, rows = terms[0][0].shape[:2]
    depth = terms[0][2][0].shape[2]
    tile = tile_of(depth)
    in_specs, args, counts = gamma_operands(terms, None, tile)
    spec = pl.BlockSpec((half, rows, tile), lambda p, s: (0, 0, p))
    aliases = None
    if before is not None:
        aliases = {len(args): 0, len(args) + 1: 1}
        in_specs += [spec, spec]
        args += before
    out = [jax.ShapeDtypeStruct((half, rows, depth), F32)] * 2
    kernel = functools.partial(gamma_kernel, counts, before is not None)
    *out, token = call(kernel, "chip_gamma", token, place, (depth // tile,), in_specs, args, [spec, spec], out, aliases, mib=36)
    return out, token


def last_gamma(token, place, which, terms, before, shape, result):
    half, rows, depth = before[0].shape
    tile = tile_of(depth)
    in_specs, args, counts = gamma_operands(terms, which, tile)
    spec = pl.BlockSpec((1, rows, tile), lambda p, s: (which, 0, p))
    in_specs += [spec, spec]
    args += before
    aliases, drop = None, 0
    if result is not None:
        aliases, drop = {len(args): 0}, 1
        in_specs.append(ANY)
        args.append(result)

    def kernel(place, *refs):
        n = len(refs) - 2
        gamma_kernel(counts, True, place, *refs[: n - drop], *refs[n:])

    out_specs = [
        pl.BlockSpec((1, rows, tile), lambda p, s: (s[1] * half + which, 0, p)),
        pl.BlockSpec((1, rows, tile), lambda p, s: (0, 0, p)),
    ]
    out = [jax.ShapeDtypeStruct(shape, F32), jax.ShapeDtypeStruct((1, rows, depth), BF16)]
    return call(kernel, "last_gamma", token, place, (depth // tile,), in_specs, args, out_specs, out, aliases, mib=24)


def place_kernel(place, received, result, out):
    del place, result
    out[...] = received[...].astype(F32)


def place_gamma(token, place, which, received, result):
    half = result.shape[0] // 2
    _, rows, depth = received.shape
    tile = rows // 2
    return call(
        place_kernel,
        "place_gamma",
        token,
        place,
        (2,),
        [pl.BlockSpec((1, tile, depth), lambda p, s: (0, p, 0)), ANY],
        [received, result],
        [pl.BlockSpec((1, tile, depth), lambda p, s: ((1 - s[1]) * half + which, p, 0))],
        [held_shape(result)],
        {1: 0},
    )


ENDS, MIDDLE = [(1, 0), (2, 3)], [(1, 2), (2, 1)]
ORDER = (
    "chip_0", "hop_1", "own_0", "combine_0", "chip_1", "gamma_0", "hop_2", "own_1", "chip_2", "own_2", "hop_3",
    "keep_3", "chip_3_0", "chip_3_1", "chip_3_2", "own_3_0", "combine_1", "own_3_1", "own_3_2", "combine_2",
    "combine_3_0", "gamma_1", "combine_3_1", "last_0", "last_1", "combine_3_2", "last_2", "place_0", "place_1",
    "place_2",
)
PIECES_2, PIECES_3, HALVES, SPLIT_1, SPLIT_2 = 1, 4, 1, False, False


class Chain:
    def __init__(self, b_occ_i, b_occ_j, eps_occ_i, eps_occ_j, eps_vir):
        self.shape = b_occ_i.shape
        self.half, self.rows = self.shape[0] // 2, self.shape[1]
        self.z, col = lax.axis_index("row"), lax.axis_index("col")
        self.x, core = col // 2, col % 2
        self.in_middle = (self.z == 1) | (self.z == 2)
        self.place = (jnp.stack([self.x, core]).astype(jnp.int32),)
        self.occ = lax.dynamic_slice_in_dim(eps_occ_i, core * self.half, self.half, 0) + eps_occ_j[self.x]
        self.eps_vir = eps_vir
        self.token = jnp.zeros(TOKEN.shape, F32)
        self.b_i = in_hbm(b_occ_i), in_hbm(self.to_core(b_occ_i))
        here = [self.to_core(b_occ_j)]
        self.block = {0: (b_occ_j, here, here)}
        self.near, self.across = self.swapped(b_occ_j, 1), self.along(b_occ_j, MIDDLE)
        self.chip, self.held, self.mirror, self.mine, self.other = {}, {}, {}, {}, {}
        self.gamma, self.result, self.received = None, None, {}

    def to_core(self, values):
        return lax.ppermute(values, "col", [(q, q ^ 1) for q in range(4)])

    def to_chip(self, values):
        return lax.ppermute(values, "col", [(q, q ^ 2) for q in range(4)])

    def along(self, values, steps):
        return lax.ppermute(values, "row", steps)

    def swapped(self, values, distance):
        return self.along(values, [(k, k ^ distance) for k in range(4)])

    def in_pieces(self, values, own_j, n_pieces):
        one = lax.dynamic_slice_in_dim(values, self.x if own_j else 1 - self.x, 1, 0)
        return [self.to_core(p) for p in jnp.split(one, n_pieces, axis=1)]

    def energies(self, distance):
        return lax.dynamic_slice_in_dim(self.eps_vir, (self.z ^ distance) * self.rows, self.rows, 0)

    def forward(self, *values):
        *out, self.token = tie(self.token, self.place, *values)
        return out

    def pass_on(self, k, which=None):
        out, self.token = pairs(self.token, self.place, self.b_i, self.block[k], False, which)
        self.chip[k, which] = self.to_chip(out)

    def own(self, k, which=None):
        last = self.chip[k, which], self.occ, self.energies(0)[:, None], self.energies(k)[None, :]
        out, self.token = pairs(self.token, self.place, self.b_i, self.block[k], True, which, last)
        self.held[k, which] = out
        self.mirror[k, which] = out if k == 0 else self.swapped(out, k)

    def combine(self, k, which=None, split=False, send=True):
        out, self.token = combine_pairs(self.token, self.place, self.held[k, which], self.mirror[k, which], split)
        outs = out if split else [out]
        keys = [(k, i) for i in range(self.half)] if split else [(k, which)]
        for key, o in zip(keys, outs):
            self.mine[key] = o
            if send:
                self.other[key] = self.to_chip(o)

    def send(self, k):
        (self.mine[k, None],) = self.forward(self.mine[k, None])
        self.other[k, None] = self.to_chip(self.mine[k, None])

    def receive(self, k):
        (self.other[k, None],) = self.forward(self.other[k, None])

    def terms(self, *keys):
        return [(self.mine[key], self.other[key], self.block[key[0]]) for key in keys]

    def add(self, *keys):
        self.gamma, self.token = chip_gamma(self.token, self.place, self.terms(*keys), self.gamma)

    def hop_1(self):
        self.near, self.across = self.forward(self.near, self.across)
        self.far_mid, self.far_end = self.along(self.near, MIDDLE), self.along(self.across, ENDS)
        near = [self.to_core(self.near)]
        self.block[1] = self.near, near, near

    def hop_2(self):
        self.far_mid, self.far_end = self.forward(self.far_mid, self.far_end)
        self.last = [self.along(p, ENDS) for p in jnp.split(self.far_mid, HALVES, axis=1)]
        far = jnp.where(self.in_middle, self.far_mid, self.far_end)
        self.block[2] = far, self.in_pieces(far, False, PIECES_2), self.in_pieces(far, True, PIECES_2)

    def hop_3(self):
        last = jnp.concatenate(self.forward(*self.last), axis=1)
        self.last = jnp.where(self.in_middle, self.across, last)
        self.block[3] = self.last, self.in_pieces(self.last, False, PIECES_3), None

    def keep_3(self):
        (last,) = self.forward(self.last)
        self.block[3] = last, self.block[3][1], self.in_pieces(last, True, PIECES_3)

    def last_sum(self, i, rounds):
        keys = [(k, i if (k, i) in self.mine else None) for k in rounds]
        self.result, theirs, self.token = last_gamma(
            self.token, self.place, i, self.terms(*keys), self.gamma, self.shape, self.result
        )
        self.received[i] = self.to_core(theirs)

    def put(self, i):
        self.result, self.token = place_gamma(self.token, self.place, i, self.received[i], self.result)

    def steps(self):
        steps = {
            "hop_1": self.hop_1, "hop_2": self.hop_2, "hop_3": self.hop_3, "keep_3": self.keep_3,
            "combine_0": functools.partial(self.combine, 0, send="send_0" not in ORDER), "send_0": functools.partial(self.send, 0),
            "combine_1": functools.partial(self.combine, 1, split=SPLIT_1), "combine_2": functools.partial(self.combine, 2, split=SPLIT_2),
            "receive_0": functools.partial(self.receive, 0), "receive_1": functools.partial(self.receive, 1),
            "receive_2": functools.partial(self.receive, 2),
            "gamma_0": functools.partial(self.add, (0, None)), "gamma_1": functools.partial(self.add, (1, None)),
            "gamma_01": functools.partial(self.add, (0, None), (1, None)),
        }
        for k in range(3):
            steps[f"chip_{k}"], steps[f"own_{k}"] = functools.partial(self.pass_on, k), functools.partial(self.own, k)
        rounds = (2, 3) if "gamma_1" in ORDER or "gamma_01" in ORDER else (1, 2, 3)
        for i in range(self.half):
            steps[f"chip_3_{i}"], steps[f"own_3_{i}"] = functools.partial(self.pass_on, 3, i), functools.partial(self.own, 3, i)
            steps[f"combine_3_{i}"] = functools.partial(self.combine, 3, i)
            steps[f"last_{i}"], steps[f"place_{i}"] = functools.partial(self.last_sum, i, rounds), functools.partial(self.put, i)
        return steps


def chain_device(b_occ_i, b_occ_j, eps_occ_i, eps_occ_j, eps_vir):
    chain = Chain(b_occ_i, b_occ_j, eps_occ_i, eps_occ_j, eps_vir)
    steps = chain.steps()
    for name in ORDER:
        steps[name]()
    return chain.result


def general_device(b_occ_i, b_occ_j, eps_occ_i, eps_occ_j, eps_vir):
    rows = b_occ_i.shape[1]
    own_energy = lax.dynamic_slice_in_dim(eps_vir, lax.axis_index("row") * rows, rows, 0)
    gathered = lax.all_gather(b_occ_j, "row", axis=1, tiled=True)
    partial_value = jnp.einsum("iap,jbp->jiab", b_occ_i, gathered, preferred_element_type=F32)
    totals = lax.psum(partial_value.astype(BF16), "col").astype(F32)
    denominator = (
        eps_occ_j[:, None, None, None]
        + eps_occ_i[None, :, None, None]
        - own_energy[None, None, :, None]
        - eps_vir[None, None, None, :]
    )
    held = (totals / denominator).astype(BF16)
    mirror = jnp.swapaxes(lax.all_to_all(held, "row", split_axis=3, concat_axis=2, tiled=True), 2, 3)
    combined = (2.0 * held.astype(F32) - mirror.astype(F32)).astype(BF16)
    return jnp.einsum("jiab,jbp->iap", combined, gathered, preferred_element_type=F32)


def solution(mesh):
    placed = (
        P("groups", "row", "col"),
        P("groups", "row", "col"),
        P("groups"),
        P("groups"),
        P("groups"),
    )
    chain = mesh.shape["row"] == 4 and mesh.shape["col"] == 4
    return jax.shard_map(
        chain_device if chain else general_device,
        mesh=mesh,
        in_specs=placed,
        out_specs=P("groups", "row", "col"),
        check_vma=False,
    )
```

```python
import functools

import jax
import jax.numpy as jnp
from jax import lax
from jax.experimental import pallas as pl
from jax.experimental.pallas import tpu as pltpu
from jax.sharding import PartitionSpec as P

F32 = jnp.float32
BF16 = jnp.bfloat16
ANY = pl.BlockSpec(memory_space=pl.ANY)
TOKEN = jax.ShapeDtypeStruct((8, 128), F32)
TILE = 256


def in_hbm(a):
    return pltpu.with_memory_space_constraint(a, pltpu.HBM)


def tile_of(size):
    return TILE if size % TILE == 0 else size


def call(kernel, name, token, place, grid, in_specs, args, out_specs, out, aliases=None, mib=8):
    def body(*refs):
        n = len(place)
        kernel(*refs[:n], *refs[n + 1 : -1])

    shift = len(place) + 1
    return pl.pallas_call(
        body,
        out_shape=(*out, TOKEN),
        grid_spec=pltpu.PrefetchScalarGridSpec(
            num_scalar_prefetch=len(place),
            grid=grid,
            in_specs=[ANY] + in_specs,
            out_specs=(*out_specs, ANY),
        ),
        input_output_aliases={k + shift: v for k, v in (aliases or {}).items()},
        compiler_params=pltpu.CompilerParams(vmem_limit_bytes=mib * 2**20),
        cost_estimate=pl.CostEstimate(flops=0, bytes_accessed=1024, transcendentals=0),
        name=name,
    )(*place, token, *args)


def tie_kernel(place, *refs):
    del place, refs


def tie(token, place, *held):
    n = len(held)
    shapes = [held_shape(h) for h in held]
    return call(tie_kernel, "tie", token, place, (1,), [ANY] * n, held, [ANY] * n, shapes, {k: k for k in range(n)})


def held_shape(a):
    return jax.ShapeDtypeStruct(a.shape, a.dtype)


def whole_block(pieces, j):
    return jnp.concatenate([p[j] for p in pieces], axis=0) if len(pieces) > 1 else pieces[0][j]


def pairs_kernel(n_place, n_pieces, has_last, first, *refs):
    place, (b_i, b_i_core, block, *rest) = refs[:n_place], refs[n_place:]
    pieces, rest, out = rest[:n_pieces], rest[n_pieces:], rest[-1]
    across = (((1,), (1,)), ((), ()))
    value = lax.dot_general(b_i[0], block[0], across, preferred_element_type=F32)
    value += lax.dot_general(b_i_core[0], whole_block(pieces, 0), across, preferred_element_type=F32)
    if has_last:
        chip, vir_a, vir_b = rest[:3]
        value = value + chip[0].astype(F32)
        value = value / ((place[1][first + pl.program_id(0)] - vir_a[...]) - vir_b[...])
    out[0] = value.astype(BF16)


def pairs(token, place, b_i, block, own_j, which=None, last=None):
    (mine, core_part), (block, passed, kept) = b_i, block
    pieces = kept if own_j else passed
    cols, depth = block.shape[1:]
    half, rows = core_part.shape[0] // 2, core_part.shape[1]
    first, count = (0, half) if which is None else which

    def j_of(s):
        return s[0] if own_j else 1 - s[0]

    one = pl.BlockSpec((1, rows, cols), lambda i, s, *_: (i, 0, 0))
    in_specs = [
        pl.BlockSpec((1, rows, depth), lambda i, s, *_: (s[1] * half + first + i, 0, 0)),
        pl.BlockSpec((1, rows, depth), lambda i, s, *_: (s[1] * half + first + i, 0, 0)),
        pl.BlockSpec((1, cols, depth), lambda i, s, *_: (j_of(s), 0, 0)),
    ]
    for p in pieces:
        one_j = p.shape[0] == 1
        in_specs.append(pl.BlockSpec((1,) + p.shape[1:], lambda i, s, *_, one_j=one_j: (0 if one_j else j_of(s), 0, 0)))
    args, name = [mine, core_part, block, *pieces], "pairs_for_chip"
    if last is not None:
        chip, occ, vir_a, vir_b = last
        place = place + (occ,)
        in_specs += [
            one,
            pl.BlockSpec((rows, 1), lambda i, s, *_: (0, 0)),
            pl.BlockSpec((1, cols), lambda i, s, *_: (0, 0)),
        ]
        args += [chip, vir_a, vir_b]
        name = "own_amplitudes"
    out = jax.ShapeDtypeStruct((count, rows, cols), BF16)
    kernel = functools.partial(pairs_kernel, len(place), len(pieces), last is not None, first)
    return call(kernel, name, token, place, (count,), in_specs, args, [one], [out], mib=24)


def combine_kernel(place, held, mirror, *outs):
    for i, out in enumerate(outs):

        @pl.when((pl.program_id(0) == i) | (len(outs) == 1))
        def _():
            out[0] = (2.0 * held[0].astype(F32) - mirror[0].astype(F32).T).astype(BF16)


def combine_pairs(token, place, held, mirror, split):
    count, rows, cols = held.shape
    spec = pl.BlockSpec((1, rows, cols), lambda i, s: (i, 0, 0))
    out_specs, out = [spec], [held_shape(held)]
    if split:
        out_specs = [pl.BlockSpec((1, rows, cols), lambda i, s: (0, 0, 0))] * count
        out = [jax.ShapeDtypeStruct((1, rows, cols), BF16)] * count
    *out, token = call(combine_kernel, "combine_pairs", token, place, (count,), [spec, spec], [held, mirror], out_specs, out, mib=12)
    return (out if split else out[0]), token


def gamma_kernel(terms, has_sum, place, *refs):
    x = place[0]
    refs, outs = list(refs[:-2]), refs[-2:]
    count, rows, tile = outs[0].shape
    held = []
    for n_passed, n_kept in terms:
        same_j, other_j, block = refs[:3]
        passed, kept = refs[3 : 3 + n_passed], refs[3 + n_passed : 3 + n_passed + n_kept]
        refs = refs[3 + n_passed + n_kept :]
        core_j = (0, 0) if n_kept else (x, 1 - x)
        held.append((same_j, (lambda block=block: block[x], lambda kept=kept or passed, j=core_j[0]: whole_block(kept, j))))
        held.append((other_j, (lambda block=block: block[1 - x], lambda passed=passed, j=core_j[1]: whole_block(passed, j))))
    for k, out in enumerate(outs):
        total = refs[k][...].reshape(count * rows, tile) if has_sum else None
        for pair, blocks in held:
            left = pair[...].reshape(count * rows, pair.shape[2])
            term = jnp.dot(left, blocks[k](), preferred_element_type=F32)
            total = term if total is None else total + term
        out[...] = total.reshape(count, rows, tile).astype(out.dtype)


def gamma_operands(terms, which, tile, half):
    in_specs, args, counts = [], [], []
    for same_j, other_j, (block, passed, kept) in terms:
        for h in (same_j, other_j):
            if which is None or h.shape[0] == 1:
                in_specs.append(pl.BlockSpec(h.shape, lambda p, s: (0, 0, 0), pipeline_mode=pl.Buffered(1)))
            else:
                at = which - (0 if h.shape[0] == half else [f for f, n in GROUPS if f <= which < f + n][0])
                in_specs.append(pl.BlockSpec((1,) + h.shape[1:], lambda p, s, at=at: (at, 0, 0)))
        kept = [] if kept is passed else kept
        blocks = [block, *passed, *kept]
        in_specs += [pl.BlockSpec(b.shape[:2] + (tile,), lambda p, s: (0, 0, p)) for b in blocks]
        args += [same_j, other_j, *blocks]
        counts.append((len(passed), len(kept)))
    return in_specs, args, counts


def chip_gamma(token, place, terms, before=None):
    half, rows = terms[0][0].shape[:2]
    depth = terms[0][2][0].shape[2]
    tile = tile_of(depth)
    in_specs, args, counts = gamma_operands(terms, None, tile, half)
    spec = pl.BlockSpec((half, rows, tile), lambda p, s: (0, 0, p))
    aliases = None
    if before is not None:
        aliases = {len(args): 0, len(args) + 1: 1}
        in_specs += [spec, spec]
        args += before
    out = [jax.ShapeDtypeStruct((half, rows, depth), F32)] * 2
    kernel = functools.partial(gamma_kernel, counts, before is not None)
    name = f"chip_gamma_{len(terms)}_{len(before or [])}"
    *out, token = call(kernel, name, token, place, (depth // tile,), in_specs, args, [spec, spec], out, aliases, mib=28 + 6 * len(terms))
    return out, token


def last_gamma(token, place, which, terms, before, shape, result):
    half, rows, depth = before[0].shape
    tile = tile_of(depth)
    in_specs, args, counts = gamma_operands(terms, which, tile, half)
    spec = pl.BlockSpec((1, rows, tile), lambda p, s: (which, 0, p))
    in_specs += [spec, spec]
    args += before
    aliases, drop = None, 0
    if result is not None:
        aliases, drop = {len(args): 0}, 1
        in_specs.append(ANY)
        args.append(result)

    def kernel(place, *refs):
        n = len(refs) - 2
        gamma_kernel(counts, True, place, *refs[: n - drop], *refs[n:])

    out_specs = [
        pl.BlockSpec((1, rows, tile), lambda p, s: (s[1] * half + which, 0, p)),
        pl.BlockSpec((1, rows, tile), lambda p, s: (0, 0, p)),
    ]
    out = [jax.ShapeDtypeStruct(shape, F32), jax.ShapeDtypeStruct((1, rows, depth), BF16)]
    return call(kernel, f"last_gamma_{len(terms)}", token, place, (depth // tile,), in_specs, args, out_specs, out, aliases, mib=24)


def place_kernel(place, received, result, out):
    del place, result
    out[...] = received[...].astype(F32)


def place_gamma(token, place, which, received, result):
    half = result.shape[0] // 2
    _, rows, depth = received.shape
    tile = rows // 2
    return call(
        place_kernel,
        "place_gamma",
        token,
        place,
        (2,),
        [pl.BlockSpec((1, tile, depth), lambda p, s: (0, p, 0)), ANY],
        [received, result],
        [pl.BlockSpec((1, tile, depth), lambda p, s: ((1 - s[1]) * half + which, p, 0))],
        [held_shape(result)],
        {1: 0},
    )


ENDS, MIDDLE = [(1, 0), (2, 3)], [(1, 2), (2, 1)]
ORDER = (
    "chip_0", "hop_1", "own_0", "combine_0", "chip_1", "gamma_0", "hop_2", "own_1", "chip_2", "own_2", "hop_3",
    "keep_3", "chip_3_0", "chip_3_1", "chip_3_2", "own_3_0", "combine_1", "own_3_1", "own_3_2", "combine_2",
    "combine_3_0", "gamma_1", "combine_3_1", "last_0", "last_1", "combine_3_2", "last_2", "place_0", "place_1",
    "place_2",
)
PIECES_2, PIECES_3, HALVES, SPLIT_1, SPLIT_2 = 2, 4, 1, False, False
GROUPS = ((0, 1), (1, 1), (2, 1))


class Chain:
    def __init__(self, b_occ_i, b_occ_j, eps_occ_i, eps_occ_j, eps_vir):
        self.shape = b_occ_i.shape
        self.half, self.rows = self.shape[0] // 2, self.shape[1]
        self.z, col = lax.axis_index("row"), lax.axis_index("col")
        self.x, core = col // 2, col % 2
        self.in_middle = (self.z == 1) | (self.z == 2)
        self.place = (jnp.stack([self.x, core]).astype(jnp.int32),)
        self.occ = lax.dynamic_slice_in_dim(eps_occ_i, core * self.half, self.half, 0) + eps_occ_j[self.x]
        self.eps_vir = eps_vir
        self.token = jnp.zeros(TOKEN.shape, F32)
        self.b_i = in_hbm(b_occ_i), in_hbm(self.to_core(b_occ_i))
        here = [self.to_core(b_occ_j)]
        self.block = {0: (b_occ_j, here, here)}
        self.near, self.across = self.swapped(b_occ_j, 1), self.along(b_occ_j, MIDDLE)
        self.chip, self.held, self.mirror, self.mine, self.other = {}, {}, {}, {}, {}
        self.gamma, self.result, self.received = None, None, {}

    def to_core(self, values):
        return lax.ppermute(values, "col", [(q, q ^ 1) for q in range(4)])

    def to_chip(self, values):
        return lax.ppermute(values, "col", [(q, q ^ 2) for q in range(4)])

    def along(self, values, steps):
        return lax.ppermute(values, "row", steps)

    def swapped(self, values, distance):
        return self.along(values, [(k, k ^ distance) for k in range(4)])

    def in_pieces(self, values, own_j, n_pieces):
        one = lax.dynamic_slice_in_dim(values, self.x if own_j else 1 - self.x, 1, 0)
        return [self.to_core(p) for p in jnp.split(one, n_pieces, axis=1)]

    def energies(self, distance):
        return lax.dynamic_slice_in_dim(self.eps_vir, (self.z ^ distance) * self.rows, self.rows, 0)

    def forward(self, *values):
        *out, self.token = tie(self.token, self.place, *values)
        return out

    def pass_on(self, k, which=None):
        out, self.token = pairs(self.token, self.place, self.b_i, self.block[k], False, which)
        self.chip[k, which] = self.to_chip(out)

    def own(self, k, which=None):
        last = self.chip[k, which], self.occ, self.energies(0)[:, None], self.energies(k)[None, :]
        out, self.token = pairs(self.token, self.place, self.b_i, self.block[k], True, which, last)
        self.held[k, which] = out
        self.mirror[k, which] = out if k == 0 else self.swapped(out, k)

    def combine(self, k, which=None, split=False, send=True):
        out, self.token = combine_pairs(self.token, self.place, self.held[k, which], self.mirror[k, which], split)
        outs = out if split else [out]
        keys = [(k, i) for i in range(self.half)] if split else [(k, which)]
        for key, o in zip(keys, outs):
            self.mine[key] = o
            if send:
                self.other[key] = self.to_chip(o)

    def send(self, k):
        (self.mine[k, None],) = self.forward(self.mine[k, None])
        self.other[k, None] = self.to_chip(self.mine[k, None])

    def receive(self, k):
        (self.other[k, None],) = self.forward(self.other[k, None])

    def terms(self, *keys):
        return [(self.mine[key], self.other[key], self.block[key[0]]) for key in keys]

    def add(self, *rounds):
        out, self.token = chip_gamma(self.token, self.place, self.terms(*((k, None) for k in rounds)), self.gamma)
        self.gamma = [in_hbm(o) for o in out]

    def hop_1(self):
        self.near, self.across = self.forward(self.near, self.across)
        self.far_mid, self.far_end = self.along(self.near, MIDDLE), self.along(self.across, ENDS)
        near = [self.to_core(self.near)]
        self.block[1] = self.near, near, near

    def hop_2(self):
        self.far_mid, self.far_end = self.forward(self.far_mid, self.far_end)
        self.last = [self.along(p, ENDS) for p in jnp.split(self.far_mid, HALVES, axis=1)]
        far = jnp.where(self.in_middle, self.far_mid, self.far_end)
        self.block[2] = far, self.in_pieces(far, False, PIECES_2), self.in_pieces(far, True, PIECES_2)

    def hop_3(self):
        last = jnp.concatenate(self.forward(*self.last), axis=1)
        self.last = jnp.where(self.in_middle, self.across, last)
        self.block[3] = self.last, self.in_pieces(self.last, False, PIECES_3), None

    def keep_3(self):
        (last,) = self.forward(self.last)
        self.block[3] = last, self.block[3][1], self.in_pieces(last, True, PIECES_3)

    def last_sum(self, i, rounds):
        group = [g for g in GROUPS if g[0] <= i < sum(g)][0]
        keys = [(k, group if k == 3 else i if (k, i) in self.mine else None) for k in rounds]
        self.result, theirs, self.token = last_gamma(
            self.token, self.place, i, self.terms(*keys), self.gamma, self.shape, self.result
        )
        self.received[i] = self.to_core(theirs)

    def put(self, i):
        self.result, self.token = place_gamma(self.token, self.place, i, self.received[i], self.result)

    def steps(self):
        steps = {
            "hop_1": self.hop_1, "hop_2": self.hop_2, "hop_3": self.hop_3, "keep_3": self.keep_3,
            "combine_0": functools.partial(self.combine, 0, send="send_0" not in ORDER), "send_0": functools.partial(self.send, 0),
            "combine_1": functools.partial(self.combine, 1, split=SPLIT_1), "combine_2": functools.partial(self.combine, 2, split=SPLIT_2),
            "receive_0": functools.partial(self.receive, 0), "receive_1": functools.partial(self.receive, 1),
            "receive_2": functools.partial(self.receive, 2),
            "gamma_0": functools.partial(self.add, 0), "gamma_1": functools.partial(self.add, 1),
            "gamma_2": functools.partial(self.add, 2), "gamma_01": functools.partial(self.add, 0, 1),
            "gamma_12": functools.partial(self.add, 1, 2), "gamma_012": functools.partial(self.add, 0, 1, 2),
        }
        for k in range(3):
            steps[f"chip_{k}"], steps[f"own_{k}"] = functools.partial(self.pass_on, k), functools.partial(self.own, k)
        added = "".join(name for name in ORDER if name.startswith("gamma"))
        rounds = [k for k in range(4) if str(k) not in added]
        for n, group in enumerate(GROUPS):
            steps[f"chip_3_{n}"], steps[f"own_3_{n}"] = functools.partial(self.pass_on, 3, group), functools.partial(self.own, 3, group)
            steps[f"combine_3_{n}"] = functools.partial(self.combine, 3, group)
        for i in range(self.half):
            steps[f"last_{i}"], steps[f"place_{i}"] = functools.partial(self.last_sum, i, rounds), functools.partial(self.put, i)
        return steps


def chain_device(b_occ_i, b_occ_j, eps_occ_i, eps_occ_j, eps_vir):
    chain = Chain(b_occ_i, b_occ_j, eps_occ_i, eps_occ_j, eps_vir)
    steps = chain.steps()
    for name in ORDER:
        steps[name]()
    return chain.result


def general_device(b_occ_i, b_occ_j, eps_occ_i, eps_occ_j, eps_vir):
    rows = b_occ_i.shape[1]
    own_energy = lax.dynamic_slice_in_dim(eps_vir, lax.axis_index("row") * rows, rows, 0)
    gathered = lax.all_gather(b_occ_j, "row", axis=1, tiled=True)
    partial_value = jnp.einsum("iap,jbp->jiab", b_occ_i, gathered, preferred_element_type=F32)
    totals = lax.psum(partial_value.astype(BF16), "col").astype(F32)
    denominator = (
        eps_occ_j[:, None, None, None]
        + eps_occ_i[None, :, None, None]
        - own_energy[None, None, :, None]
        - eps_vir[None, None, None, :]
    )
    held = (totals / denominator).astype(BF16)
    mirror = jnp.swapaxes(lax.all_to_all(held, "row", split_axis=3, concat_axis=2, tiled=True), 2, 3)
    combined = (2.0 * held.astype(F32) - mirror.astype(F32)).astype(BF16)
    return jnp.einsum("jiab,jbp->iap", combined, gathered, preferred_element_type=F32)


def solution(mesh):
    placed = (
        P("groups", "row", "col"),
        P("groups", "row", "col"),
        P("groups"),
        P("groups"),
        P("groups"),
    )
    chain = mesh.shape["row"] == 4 and mesh.shape["col"] == 4
    return jax.shard_map(
        chain_device if chain else general_device,
        mesh=mesh,
        in_specs=placed,
        out_specs=P("groups", "row", "col"),
        check_vma=False,
    )
```

```python
import functools

import jax
import jax.numpy as jnp
from jax import lax
from jax.experimental import pallas as pl
from jax.experimental.pallas import tpu as pltpu
from jax.sharding import PartitionSpec as P

F32 = jnp.float32
BF16 = jnp.bfloat16
ANY = pl.BlockSpec(memory_space=pl.ANY)
TOKEN = jax.ShapeDtypeStruct((8, 128), F32)
TILE = 256


def in_hbm(a):
    return pltpu.with_memory_space_constraint(a, pltpu.HBM)


def tile_of(size):
    return TILE if size % TILE == 0 else size


def call(kernel, name, token, place, grid, in_specs, args, out_specs, out, aliases=None, mib=8):
    def body(*refs):
        n = len(place)
        kernel(*refs[:n], *refs[n + 1 : -1])

    shift = len(place) + 1
    return pl.pallas_call(
        body,
        out_shape=(*out, TOKEN),
        grid_spec=pltpu.PrefetchScalarGridSpec(
            num_scalar_prefetch=len(place),
            grid=grid,
            in_specs=[ANY] + in_specs,
            out_specs=(*out_specs, ANY),
        ),
        input_output_aliases={k + shift: v for k, v in (aliases or {}).items()},
        compiler_params=pltpu.CompilerParams(vmem_limit_bytes=mib * 2**20),
        cost_estimate=pl.CostEstimate(flops=0, bytes_accessed=1024, transcendentals=0),
        name=name,
    )(*place, token, *args)


def tie_kernel(place, *refs):
    del place, refs


def tie(token, place, *held):
    n = len(held)
    shapes = [held_shape(h) for h in held]
    return call(tie_kernel, "tie", token, place, (1,), [ANY] * n, held, [ANY] * n, shapes, {k: k for k in range(n)})


def held_shape(a):
    return jax.ShapeDtypeStruct(a.shape, a.dtype)


def whole_block(pieces, j):
    return jnp.concatenate([p[j] for p in pieces], axis=0) if len(pieces) > 1 else pieces[0][j]


def pairs_kernel(n_place, n_pieces, has_last, first, *refs):
    place, (b_i, b_i_core, block, *rest) = refs[:n_place], refs[n_place:]
    pieces, rest, out = rest[:n_pieces], rest[n_pieces:], rest[-1]
    across = (((1,), (1,)), ((), ()))
    value = lax.dot_general(b_i[0], block[0], across, preferred_element_type=F32)
    value += lax.dot_general(b_i_core[0], whole_block(pieces, 0), across, preferred_element_type=F32)
    if has_last:
        chip, vir_a, vir_b = rest[:3]
        value = value + chip[0].astype(F32)
        value = value / ((place[1][first + pl.program_id(0)] - vir_a[...]) - vir_b[...])
    out[0] = value.astype(BF16)


def pairs(token, place, b_i, block, own_j, which=None, last=None):
    (mine, core_part), (block, passed, kept) = b_i, block
    pieces = kept if own_j else passed
    cols, depth = block.shape[1:]
    half, rows = core_part.shape[0] // 2, core_part.shape[1]
    first, count = (0, half) if which is None else which

    def j_of(s):
        return s[0] if own_j else 1 - s[0]

    one = pl.BlockSpec((1, rows, cols), lambda i, s, *_: (i, 0, 0))
    in_specs = [
        pl.BlockSpec((1, rows, depth), lambda i, s, *_: (s[1] * half + first + i, 0, 0)),
        pl.BlockSpec((1, rows, depth), lambda i, s, *_: (s[1] * half + first + i, 0, 0)),
        pl.BlockSpec((1, cols, depth), lambda i, s, *_: (j_of(s), 0, 0)),
    ]
    for p in pieces:
        one_j = p.shape[0] == 1
        in_specs.append(pl.BlockSpec((1,) + p.shape[1:], lambda i, s, *_, one_j=one_j: (0 if one_j else j_of(s), 0, 0)))
    args, name = [mine, core_part, block, *pieces], "pairs_for_chip"
    if last is not None:
        chip, occ, vir_a, vir_b = last
        place = place + (occ,)
        in_specs += [
            one,
            pl.BlockSpec((rows, 1), lambda i, s, *_: (0, 0)),
            pl.BlockSpec((1, cols), lambda i, s, *_: (0, 0)),
        ]
        args += [chip, vir_a, vir_b]
        name = "own_amplitudes"
    out = jax.ShapeDtypeStruct((count, rows, cols), BF16)
    kernel = functools.partial(pairs_kernel, len(place), len(pieces), last is not None, first)
    return call(kernel, name, token, place, (count,), in_specs, args, [one], [out], mib=24)


def combine_kernel(place, held, mirror, *outs):
    for i, out in enumerate(outs):

        @pl.when((pl.program_id(0) == i) | (len(outs) == 1))
        def _():
            out[0] = (2.0 * held[0].astype(F32) - mirror[0].astype(F32).T).astype(BF16)


def combine_pairs(token, place, held, mirror, split):
    count, rows, cols = held.shape
    spec = pl.BlockSpec((1, rows, cols), lambda i, s: (i, 0, 0))
    out_specs, out = [spec], [held_shape(held)]
    if split:
        out_specs = [pl.BlockSpec((1, rows, cols), lambda i, s: (0, 0, 0))] * count
        out = [jax.ShapeDtypeStruct((1, rows, cols), BF16)] * count
    *out, token = call(combine_kernel, "combine_pairs", token, place, (count,), [spec, spec], [held, mirror], out_specs, out, mib=12)
    return (out if split else out[0]), token


def gamma_kernel(terms, has_sum, place, *refs):
    x = place[0]
    refs, outs = list(refs[:-2]), refs[-2:]
    count, rows, tile = outs[0].shape
    held = []
    for n_passed, n_kept in terms:
        same_j, other_j, block = refs[:3]
        passed, kept = refs[3 : 3 + n_passed], refs[3 + n_passed : 3 + n_passed + n_kept]
        refs = refs[3 + n_passed + n_kept :]
        core_j = (0, 0) if n_kept else (x, 1 - x)
        held.append((same_j, (lambda block=block: block[x], lambda kept=kept or passed, j=core_j[0]: whole_block(kept, j))))
        held.append((other_j, (lambda block=block: block[1 - x], lambda passed=passed, j=core_j[1]: whole_block(passed, j))))
    for k, out in enumerate(outs):
        total = refs[k][...].reshape(count * rows, tile) if has_sum else None
        for pair, blocks in held:
            left = pair[...].reshape(count * rows, pair.shape[2])
            term = jnp.dot(left, blocks[k](), preferred_element_type=F32)
            total = term if total is None else total + term
        out[...] = total.reshape(count, rows, tile).astype(out.dtype)


def gamma_operands(terms, which, tile, half):
    in_specs, args, counts = [], [], []
    for same_j, other_j, (block, passed, kept) in terms:
        for h in (same_j, other_j):
            if which is None or h.shape[0] == 1:
                in_specs.append(pl.BlockSpec(h.shape, lambda p, s: (0, 0, 0), pipeline_mode=pl.Buffered(1)))
            else:
                at = which - (0 if h.shape[0] == half else [f for f, n in GROUPS if f <= which < f + n][0])
                in_specs.append(pl.BlockSpec((1,) + h.shape[1:], lambda p, s, at=at: (at, 0, 0)))
        kept = [] if kept is passed else kept
        blocks = [block, *passed, *kept]
        in_specs += [pl.BlockSpec(b.shape[:2] + (tile,), lambda p, s: (0, 0, p)) for b in blocks]
        args += [same_j, other_j, *blocks]
        counts.append((len(passed), len(kept)))
    return in_specs, args, counts


def chip_gamma(token, place, terms, before=None):
    half, rows = terms[0][0].shape[:2]
    depth = terms[0][2][0].shape[2]
    tile = tile_of(depth)
    in_specs, args, counts = gamma_operands(terms, None, tile, half)
    spec = pl.BlockSpec((half, rows, tile), lambda p, s: (0, 0, p))
    aliases = None
    if before is not None:
        aliases = {len(args): 0, len(args) + 1: 1}
        in_specs += [spec, spec]
        args += before
    out = [jax.ShapeDtypeStruct((half, rows, depth), F32)] * 2
    kernel = functools.partial(gamma_kernel, counts, before is not None)
    name = f"chip_gamma_{len(terms)}_{len(before or [])}"
    *out, token = call(kernel, name, token, place, (depth // tile,), in_specs, args, [spec, spec], out, aliases, mib=28 + 6 * len(terms))
    return out, token


def last_gamma(token, place, which, terms, before, shape, result):
    half, rows, depth = before[0].shape
    tile = tile_of(depth)
    in_specs, args, counts = gamma_operands(terms, which, tile, half)
    spec = pl.BlockSpec((1, rows, tile), lambda p, s: (which, 0, p))
    in_specs += [spec, spec]
    args += before
    aliases, drop = None, 0
    if result is not None:
        aliases, drop = {len(args): 0}, 1
        in_specs.append(ANY)
        args.append(result)

    def kernel(place, *refs):
        n = len(refs) - 2
        gamma_kernel(counts, True, place, *refs[: n - drop], *refs[n:])

    out_specs = [
        pl.BlockSpec((1, rows, tile), lambda p, s: (s[1] * half + which, 0, p)),
        pl.BlockSpec((1, rows, tile), lambda p, s: (0, 0, p)),
    ]
    out = [jax.ShapeDtypeStruct(shape, F32), jax.ShapeDtypeStruct((1, rows, depth), BF16)]
    return call(kernel, f"last_gamma_{len(terms)}", token, place, (depth // tile,), in_specs, args, out_specs, out, aliases, mib=24)


def place_kernel(place, received, result, out):
    del place, result
    out[...] = received[...].astype(F32)


def place_gamma(token, place, which, received, result):
    half = result.shape[0] // 2
    _, rows, depth = received.shape
    tile = rows // 2
    return call(
        place_kernel,
        "place_gamma",
        token,
        place,
        (2,),
        [pl.BlockSpec((1, tile, depth), lambda p, s: (0, p, 0)), ANY],
        [received, result],
        [pl.BlockSpec((1, tile, depth), lambda p, s: ((1 - s[1]) * half + which, p, 0))],
        [held_shape(result)],
        {1: 0},
    )


ENDS, MIDDLE = [(1, 0), (2, 3)], [(1, 2), (2, 1)]
ORDER = (
    "chip_0", "hop_1", "own_0", "combine_0", "chip_1", "gamma_0", "hop_2", "own_1", "chip_2", "own_2", "hop_3",
    "keep_3", "chip_3_0", "chip_3_1", "chip_3_2", "own_3_0", "combine_1", "own_3_1", "own_3_2", "combine_2",
    "receive_1", "gamma_1", "combine_3_0", "receive_2", "combine_3_1", "last_0", "combine_3_2", "last_1", "last_2",
    "place_0", "place_1", "place_2",
)
PIECES_2, PIECES_3, HALVES, SPLIT_1, SPLIT_2 = 2, 4, 1, False, False
GROUPS = ((0, 1), (1, 1), (2, 1))


class Chain:
    def __init__(self, b_occ_i, b_occ_j, eps_occ_i, eps_occ_j, eps_vir):
        self.shape = b_occ_i.shape
        self.half, self.rows = self.shape[0] // 2, self.shape[1]
        self.z, col = lax.axis_index("row"), lax.axis_index("col")
        self.x, core = col // 2, col % 2
        self.in_middle = (self.z == 1) | (self.z == 2)
        self.place = (jnp.stack([self.x, core]).astype(jnp.int32),)
        self.occ = lax.dynamic_slice_in_dim(eps_occ_i, core * self.half, self.half, 0) + eps_occ_j[self.x]
        self.eps_vir = eps_vir
        self.token = jnp.zeros(TOKEN.shape, F32)
        self.b_i = in_hbm(b_occ_i), in_hbm(self.to_core(b_occ_i))
        here = [self.to_core(b_occ_j)]
        self.block = {0: (b_occ_j, here, here)}
        self.near, self.across = self.swapped(b_occ_j, 1), self.along(b_occ_j, MIDDLE)
        self.chip, self.held, self.mirror, self.mine, self.other = {}, {}, {}, {}, {}
        self.gamma, self.result, self.received = None, None, {}

    def to_core(self, values):
        return lax.ppermute(values, "col", [(q, q ^ 1) for q in range(4)])

    def to_chip(self, values):
        return lax.ppermute(values, "col", [(q, q ^ 2) for q in range(4)])

    def along(self, values, steps):
        return lax.ppermute(values, "row", steps)

    def swapped(self, values, distance):
        return self.along(values, [(k, k ^ distance) for k in range(4)])

    def in_pieces(self, values, own_j, n_pieces):
        one = lax.dynamic_slice_in_dim(values, self.x if own_j else 1 - self.x, 1, 0)
        return [self.to_core(p) for p in jnp.split(one, n_pieces, axis=1)]

    def energies(self, distance):
        return lax.dynamic_slice_in_dim(self.eps_vir, (self.z ^ distance) * self.rows, self.rows, 0)

    def forward(self, *values):
        *out, self.token = tie(self.token, self.place, *values)
        return out

    def pass_on(self, k, which=None):
        out, self.token = pairs(self.token, self.place, self.b_i, self.block[k], False, which)
        self.chip[k, which] = self.to_chip(out)

    def own(self, k, which=None):
        last = self.chip[k, which], self.occ, self.energies(0)[:, None], self.energies(k)[None, :]
        out, self.token = pairs(self.token, self.place, self.b_i, self.block[k], True, which, last)
        self.held[k, which] = out
        self.mirror[k, which] = out if k == 0 else self.swapped(out, k)

    def combine(self, k, which=None, split=False, send=True):
        out, self.token = combine_pairs(self.token, self.place, self.held[k, which], self.mirror[k, which], split)
        outs = out if split else [out]
        keys = [(k, i) for i in range(self.half)] if split else [(k, which)]
        for key, o in zip(keys, outs):
            self.mine[key] = o
            if send:
                self.other[key] = self.to_chip(o)

    def send(self, k):
        (self.mine[k, None],) = self.forward(self.mine[k, None])
        self.other[k, None] = self.to_chip(self.mine[k, None])

    def receive(self, k):
        (self.other[k, None],) = self.forward(self.other[k, None])

    def terms(self, *keys):
        return [(self.mine[key], self.other[key], self.block[key[0]]) for key in keys]

    def add(self, *rounds):
        out, self.token = chip_gamma(self.token, self.place, self.terms(*((k, None) for k in rounds)), self.gamma)
        self.gamma = [in_hbm(o) for o in out]

    def hop_1(self):
        self.near, self.across = self.forward(self.near, self.across)
        self.far_mid, self.far_end = self.along(self.near, MIDDLE), self.along(self.across, ENDS)
        near = [self.to_core(self.near)]
        self.block[1] = self.near, near, near

    def hop_2(self):
        self.far_mid, self.far_end = self.forward(self.far_mid, self.far_end)
        self.last = [self.along(p, ENDS) for p in jnp.split(self.far_mid, HALVES, axis=1)]
        far = jnp.where(self.in_middle, self.far_mid, self.far_end)
        self.block[2] = far, self.in_pieces(far, False, PIECES_2), self.in_pieces(far, True, PIECES_2)

    def hop_3(self):
        last = jnp.concatenate(self.forward(*self.last), axis=1)
        self.last = jnp.where(self.in_middle, self.across, last)
        self.block[3] = self.last, self.in_pieces(self.last, False, PIECES_3), None

    def keep_3(self):
        (last,) = self.forward(self.last)
        self.block[3] = last, self.block[3][1], self.in_pieces(last, True, PIECES_3)

    def last_sum(self, i, rounds):
        group = [g for g in GROUPS if g[0] <= i < sum(g)][0]
        keys = [(k, group if k == 3 else i if (k, i) in self.mine else None) for k in rounds]
        self.result, theirs, self.token = last_gamma(
            self.token, self.place, i, self.terms(*keys), self.gamma, self.shape, self.result
        )
        self.received[i] = self.to_core(theirs)

    def put(self, i):
        self.result, self.token = place_gamma(self.token, self.place, i, self.received[i], self.result)

    def steps(self):
        steps = {
            "hop_1": self.hop_1, "hop_2": self.hop_2, "hop_3": self.hop_3, "keep_3": self.keep_3,
            "combine_0": functools.partial(self.combine, 0, send="send_0" not in ORDER), "send_0": functools.partial(self.send, 0),
            "combine_1": functools.partial(self.combine, 1, split=SPLIT_1), "combine_2": functools.partial(self.combine, 2, split=SPLIT_2),
            "receive_0": functools.partial(self.receive, 0), "receive_1": functools.partial(self.receive, 1),
            "receive_2": functools.partial(self.receive, 2),
            "gamma_0": functools.partial(self.add, 0), "gamma_1": functools.partial(self.add, 1),
            "gamma_2": functools.partial(self.add, 2), "gamma_01": functools.partial(self.add, 0, 1),
            "gamma_12": functools.partial(self.add, 1, 2), "gamma_012": functools.partial(self.add, 0, 1, 2),
        }
        for k in range(3):
            steps[f"chip_{k}"], steps[f"own_{k}"] = functools.partial(self.pass_on, k), functools.partial(self.own, k)
        added = "".join(name for name in ORDER if name.startswith("gamma"))
        rounds = [k for k in range(4) if str(k) not in added]
        for n, group in enumerate(GROUPS):
            steps[f"chip_3_{n}"], steps[f"own_3_{n}"] = functools.partial(self.pass_on, 3, group), functools.partial(self.own, 3, group)
            steps[f"combine_3_{n}"] = functools.partial(self.combine, 3, group)
        for i in range(self.half):
            steps[f"last_{i}"], steps[f"place_{i}"] = functools.partial(self.last_sum, i, rounds), functools.partial(self.put, i)
        return steps


def chain_device(b_occ_i, b_occ_j, eps_occ_i, eps_occ_j, eps_vir):
    chain = Chain(b_occ_i, b_occ_j, eps_occ_i, eps_occ_j, eps_vir)
    steps = chain.steps()
    for name in ORDER:
        steps[name]()
    return chain.result


def general_device(b_occ_i, b_occ_j, eps_occ_i, eps_occ_j, eps_vir):
    rows = b_occ_i.shape[1]
    own_energy = lax.dynamic_slice_in_dim(eps_vir, lax.axis_index("row") * rows, rows, 0)
    gathered = lax.all_gather(b_occ_j, "row", axis=1, tiled=True)
    partial_value = jnp.einsum("iap,jbp->jiab", b_occ_i, gathered, preferred_element_type=F32)
    totals = lax.psum(partial_value.astype(BF16), "col").astype(F32)
    denominator = (
        eps_occ_j[:, None, None, None]
        + eps_occ_i[None, :, None, None]
        - own_energy[None, None, :, None]
        - eps_vir[None, None, None, :]
    )
    held = (totals / denominator).astype(BF16)
    mirror = jnp.swapaxes(lax.all_to_all(held, "row", split_axis=3, concat_axis=2, tiled=True), 2, 3)
    combined = (2.0 * held.astype(F32) - mirror.astype(F32)).astype(BF16)
    return jnp.einsum("jiab,jbp->iap", combined, gathered, preferred_element_type=F32)


def solution(mesh):
    placed = (
        P("groups", "row", "col"),
        P("groups", "row", "col"),
        P("groups"),
        P("groups"),
        P("groups"),
    )
    chain = mesh.shape["row"] == 4 and mesh.shape["col"] == 4
    return jax.shard_map(
        chain_device if chain else general_device,
        mesh=mesh,
        in_specs=placed,
        out_specs=P("groups", "row", "col"),
        check_vma=False,
    )
```

```python
import functools

import jax
import jax.numpy as jnp
from jax import lax
from jax.experimental import pallas as pl
from jax.experimental.pallas import tpu as pltpu
from jax.sharding import PartitionSpec as P

F32 = jnp.float32
BF16 = jnp.bfloat16
ANY = pl.BlockSpec(memory_space=pl.ANY)
TOKEN = jax.ShapeDtypeStruct((8, 128), F32)
TILE = 256


def in_hbm(a):
    return pltpu.with_memory_space_constraint(a, pltpu.HBM)


def tile_of(size):
    return TILE if size % TILE == 0 else size


def call(kernel, name, token, place, grid, in_specs, args, out_specs, out, aliases=None, mib=8):
    def body(*refs):
        n = len(place)
        kernel(*refs[:n], *refs[n + 1 : -1])

    shift = len(place) + 1
    return pl.pallas_call(
        body,
        out_shape=(*out, TOKEN),
        grid_spec=pltpu.PrefetchScalarGridSpec(
            num_scalar_prefetch=len(place),
            grid=grid,
            in_specs=[ANY] + in_specs,
            out_specs=(*out_specs, ANY),
        ),
        input_output_aliases={k + shift: v for k, v in (aliases or {}).items()},
        compiler_params=pltpu.CompilerParams(vmem_limit_bytes=mib * 2**20),
        cost_estimate=pl.CostEstimate(flops=0, bytes_accessed=1024, transcendentals=0),
        name=name,
    )(*place, token, *args)


def tie_kernel(place, *refs):
    del place, refs


def tie(token, place, *held):
    n = len(held)
    shapes = [held_shape(h) for h in held]
    return call(tie_kernel, "tie", token, place, (1,), [ANY] * n, held, [ANY] * n, shapes, {k: k for k in range(n)})


def held_shape(a):
    return jax.ShapeDtypeStruct(a.shape, a.dtype)


def whole_block(pieces, j):
    return jnp.concatenate([p[j] for p in pieces], axis=0) if len(pieces) > 1 else pieces[0][j]


def pairs_kernel(n_place, n_pieces, has_last, first, *refs):
    place, (b_i, b_i_core, block, *rest) = refs[:n_place], refs[n_place:]
    pieces, rest, out = rest[:n_pieces], rest[n_pieces:], rest[-1]
    across = (((1,), (1,)), ((), ()))
    value = lax.dot_general(b_i[0], block[0], across, preferred_element_type=F32)
    value += lax.dot_general(b_i_core[0], whole_block(pieces, 0), across, preferred_element_type=F32)
    if has_last:
        chip, vir_a, vir_b = rest[:3]
        value = value + chip[0].astype(F32)
        value = value / ((place[1][first + pl.program_id(0)] - vir_a[...]) - vir_b[...])
    out[0] = value.astype(BF16)


def pairs(token, place, b_i, block, own_j, which=None, last=None):
    (mine, core_part), (block, passed, kept) = b_i, block
    pieces = kept if own_j else passed
    cols, depth = block.shape[1:]
    half, rows = core_part.shape[0] // 2, core_part.shape[1]
    first, count = (0, half) if which is None else which

    def j_of(s):
        return s[0] if own_j else 1 - s[0]

    one = pl.BlockSpec((1, rows, cols), lambda i, s, *_: (i, 0, 0))
    in_specs = [
        pl.BlockSpec((1, rows, depth), lambda i, s, *_: (s[1] * half + first + i, 0, 0)),
        pl.BlockSpec((1, rows, depth), lambda i, s, *_: (s[1] * half + first + i, 0, 0)),
        pl.BlockSpec((1, cols, depth), lambda i, s, *_: (j_of(s), 0, 0)),
    ]
    for p in pieces:
        one_j = p.shape[0] == 1
        in_specs.append(pl.BlockSpec((1,) + p.shape[1:], lambda i, s, *_, one_j=one_j: (0 if one_j else j_of(s), 0, 0)))
    args, name = [mine, core_part, block, *pieces], "pairs_for_chip"
    if last is not None:
        chip, occ, vir_a, vir_b = last
        place = place + (occ,)
        in_specs += [
            one,
            pl.BlockSpec((rows, 1), lambda i, s, *_: (0, 0)),
            pl.BlockSpec((1, cols), lambda i, s, *_: (0, 0)),
        ]
        args += [chip, vir_a, vir_b]
        name = "own_amplitudes"
    out = jax.ShapeDtypeStruct((count, rows, cols), BF16)
    kernel = functools.partial(pairs_kernel, len(place), len(pieces), last is not None, first)
    return call(kernel, name, token, place, (count,), in_specs, args, [one], [out], mib=24)


def combine_kernel(place, held, mirror, *outs):
    for i, out in enumerate(outs):

        @pl.when((pl.program_id(0) == i) | (len(outs) == 1))
        def _():
            out[0] = (2.0 * held[0].astype(F32) - mirror[0].astype(F32).T).astype(BF16)


def combine_pairs(token, place, held, mirror, split):
    count, rows, cols = held.shape
    spec = pl.BlockSpec((1, rows, cols), lambda i, s: (i, 0, 0))
    out_specs, out = [spec], [held_shape(held)]
    if split:
        out_specs = [pl.BlockSpec((1, rows, cols), lambda i, s: (0, 0, 0))] * count
        out = [jax.ShapeDtypeStruct((1, rows, cols), BF16)] * count
    *out, token = call(combine_kernel, "combine_pairs", token, place, (count,), [spec, spec], [held, mirror], out_specs, out, mib=12)
    return (out if split else out[0]), token


def gamma_kernel(terms, has_sum, place, *refs):
    x = place[0]
    refs, outs = list(refs[:-2]), refs[-2:]
    count, rows, tile = outs[0].shape
    held = []
    for n_passed, n_kept in terms:
        same_j, other_j, block = refs[:3]
        passed, kept = refs[3 : 3 + n_passed], refs[3 + n_passed : 3 + n_passed + n_kept]
        refs = refs[3 + n_passed + n_kept :]
        core_j = (0, 0) if n_kept else (x, 1 - x)
        held.append((same_j, (lambda block=block: block[x], lambda kept=kept or passed, j=core_j[0]: whole_block(kept, j))))
        held.append((other_j, (lambda block=block: block[1 - x], lambda passed=passed, j=core_j[1]: whole_block(passed, j))))
    for k, out in enumerate(outs):
        total = refs[k][...].reshape(count * rows, tile) if has_sum else None
        for pair, blocks in held:
            left = pair[...].reshape(count * rows, pair.shape[2])
            term = jnp.dot(left, blocks[k](), preferred_element_type=F32)
            total = term if total is None else total + term
        out[...] = total.reshape(count, rows, tile).astype(out.dtype)


def gamma_operands(terms, which, tile, half):
    in_specs, args, counts = [], [], []
    for same_j, other_j, (block, passed, kept) in terms:
        for h in (same_j, other_j):
            if which is None or h.shape[0] == 1:
                in_specs.append(pl.BlockSpec(h.shape, lambda p, s: (0, 0, 0), pipeline_mode=pl.Buffered(1)))
            else:
                at = which - (0 if h.shape[0] == half else [f for f, n in GROUPS if f <= which < f + n][0])
                in_specs.append(pl.BlockSpec((1,) + h.shape[1:], lambda p, s, at=at: (at, 0, 0)))
        kept = [] if kept is passed else kept
        blocks = [block, *passed, *kept]
        in_specs += [pl.BlockSpec(b.shape[:2] + (tile,), lambda p, s: (0, 0, p)) for b in blocks]
        args += [same_j, other_j, *blocks]
        counts.append((len(passed), len(kept)))
    return in_specs, args, counts


def chip_gamma(token, place, terms, before=None):
    half, rows = terms[0][0].shape[:2]
    depth = terms[0][2][0].shape[2]
    tile = tile_of(depth)
    in_specs, args, counts = gamma_operands(terms, None, tile, half)
    spec = pl.BlockSpec((half, rows, tile), lambda p, s: (0, 0, p))
    aliases = None
    if before is not None:
        aliases = {len(args): 0, len(args) + 1: 1}
        in_specs += [spec, spec]
        args += before
    out = [jax.ShapeDtypeStruct((half, rows, depth), F32)] * 2
    kernel = functools.partial(gamma_kernel, counts, before is not None)
    name = f"chip_gamma_{len(terms)}_{len(before or [])}"
    *out, token = call(kernel, name, token, place, (depth // tile,), in_specs, args, [spec, spec], out, aliases, mib=28 + 6 * len(terms))
    return out, token


def last_gamma(token, place, which, terms, before, shape, result):
    half, rows, depth = before[0].shape
    tile = 2 * TILE if depth % (2 * TILE) == 0 else depth
    in_specs, args, counts = gamma_operands(terms, which, tile, half)
    spec = pl.BlockSpec((1, rows, tile), lambda p, s: (which, 0, p))
    in_specs += [spec, spec]
    args += before
    aliases, drop = None, 0
    if result is not None:
        aliases, drop = {len(args): 0}, 1
        in_specs.append(ANY)
        args.append(result)

    def kernel(place, *refs):
        n = len(refs) - 2
        gamma_kernel(counts, True, place, *refs[: n - drop], *refs[n:])

    out_specs = [
        pl.BlockSpec((1, rows, tile), lambda p, s: (s[1] * half + which, 0, p)),
        pl.BlockSpec((1, rows, tile), lambda p, s: (0, 0, p)),
    ]
    out = [jax.ShapeDtypeStruct(shape, F32), jax.ShapeDtypeStruct((1, rows, depth), BF16)]
    return call(kernel, f"last_gamma_{len(terms)}", token, place, (depth // tile,), in_specs, args, out_specs, out, aliases, mib=36)


def place_kernel(place, received, result, out):
    del place, result
    out[...] = received[...].astype(F32)


def place_gamma(token, place, which, received, result):
    half = result.shape[0] // 2
    _, rows, depth = received.shape
    tile = rows // 2
    return call(
        place_kernel,
        "place_gamma",
        token,
        place,
        (2,),
        [pl.BlockSpec((1, tile, depth), lambda p, s: (0, p, 0)), ANY],
        [received, result],
        [pl.BlockSpec((1, tile, depth), lambda p, s: ((1 - s[1]) * half + which, p, 0))],
        [held_shape(result)],
        {1: 0},
    )


ENDS, MIDDLE = [(1, 0), (2, 3)], [(1, 2), (2, 1)]
ORDER = (
    "chip_0", "hop_1", "own_0", "combine_0", "chip_1", "gamma_0", "hop_2", "own_1", "chip_2", "own_2", "hop_3",
    "keep_3", "chip_3_0", "chip_3_1", "chip_3_2", "own_3_0", "combine_1", "own_3_1", "own_3_2", "combine_2",
    "receive_1", "gamma_1", "combine_3_0", "receive_2", "combine_3_1", "last_0", "combine_3_2", "last_1", "last_2",
    "place_0", "place_1", "place_2",
)
PIECES_2, PIECES_3, HALVES, SPLIT_1, SPLIT_2 = 2, 4, 1, False, False
GROUPS = ((0, 1), (1, 1), (2, 1))


class Chain:
    def __init__(self, b_occ_i, b_occ_j, eps_occ_i, eps_occ_j, eps_vir):
        self.shape = b_occ_i.shape
        self.half, self.rows = self.shape[0] // 2, self.shape[1]
        self.z, col = lax.axis_index("row"), lax.axis_index("col")
        self.x, core = col // 2, col % 2
        self.in_middle = (self.z == 1) | (self.z == 2)
        self.place = (jnp.stack([self.x, core]).astype(jnp.int32),)
        self.occ = lax.dynamic_slice_in_dim(eps_occ_i, core * self.half, self.half, 0) + eps_occ_j[self.x]
        self.eps_vir = eps_vir
        self.token = jnp.zeros(TOKEN.shape, F32)
        self.b_i = in_hbm(b_occ_i), in_hbm(self.to_core(b_occ_i))
        here = [self.to_core(b_occ_j)]
        self.block = {0: (b_occ_j, here, here)}
        self.near, self.across = self.swapped(b_occ_j, 1), self.along(b_occ_j, MIDDLE)
        self.chip, self.held, self.mirror, self.mine, self.other = {}, {}, {}, {}, {}
        self.gamma, self.result, self.received = None, None, {}

    def to_core(self, values):
        return lax.ppermute(values, "col", [(q, q ^ 1) for q in range(4)])

    def to_chip(self, values):
        return lax.ppermute(values, "col", [(q, q ^ 2) for q in range(4)])

    def along(self, values, steps):
        return lax.ppermute(values, "row", steps)

    def swapped(self, values, distance):
        return self.along(values, [(k, k ^ distance) for k in range(4)])

    def in_pieces(self, values, own_j, n_pieces):
        one = lax.dynamic_slice_in_dim(values, self.x if own_j else 1 - self.x, 1, 0)
        return [self.to_core(p) for p in jnp.split(one, n_pieces, axis=1)]

    def energies(self, distance):
        return lax.dynamic_slice_in_dim(self.eps_vir, (self.z ^ distance) * self.rows, self.rows, 0)

    def forward(self, *values):
        *out, self.token = tie(self.token, self.place, *values)
        return out

    def pass_on(self, k, which=None):
        out, self.token = pairs(self.token, self.place, self.b_i, self.block[k], False, which)
        self.chip[k, which] = self.to_chip(out)

    def own(self, k, which=None):
        last = self.chip[k, which], self.occ, self.energies(0)[:, None], self.energies(k)[None, :]
        out, self.token = pairs(self.token, self.place, self.b_i, self.block[k], True, which, last)
        self.held[k, which] = out
        self.mirror[k, which] = out if k == 0 else self.swapped(out, k)

    def combine(self, k, which=None, split=False, send=True):
        out, self.token = combine_pairs(self.token, self.place, self.held[k, which], self.mirror[k, which], split)
        outs = out if split else [out]
        keys = [(k, i) for i in range(self.half)] if split else [(k, which)]
        for key, o in zip(keys, outs):
            self.mine[key] = o
            if send:
                self.other[key] = self.to_chip(o)

    def send(self, k):
        (self.mine[k, None],) = self.forward(self.mine[k, None])
        self.other[k, None] = self.to_chip(self.mine[k, None])

    def receive(self, k):
        (self.other[k, None],) = self.forward(self.other[k, None])

    def terms(self, *keys):
        return [(self.mine[key], self.other[key], self.block[key[0]]) for key in keys]

    def add(self, *rounds):
        out, self.token = chip_gamma(self.token, self.place, self.terms(*((k, None) for k in rounds)), self.gamma)
        self.gamma = [in_hbm(o) for o in out]

    def hop_1(self):
        self.near, self.across = self.forward(self.near, self.across)
        self.far_mid, self.far_end = self.along(self.near, MIDDLE), self.along(self.across, ENDS)
        near = [self.to_core(self.near)]
        self.block[1] = self.near, near, near

    def hop_2(self):
        self.far_mid, self.far_end = self.forward(self.far_mid, self.far_end)
        self.last = [self.along(p, ENDS) for p in jnp.split(self.far_mid, HALVES, axis=1)]
        far = jnp.where(self.in_middle, self.far_mid, self.far_end)
        self.block[2] = far, self.in_pieces(far, False, PIECES_2), self.in_pieces(far, True, PIECES_2)

    def hop_3(self):
        last = jnp.concatenate(self.forward(*self.last), axis=1)
        self.last = jnp.where(self.in_middle, self.across, last)
        self.block[3] = self.last, self.in_pieces(self.last, False, PIECES_3), None

    def keep_3(self):
        (last,) = self.forward(self.last)
        self.block[3] = last, self.block[3][1], self.in_pieces(last, True, PIECES_3)

    def last_sum(self, i, rounds):
        group = [g for g in GROUPS if g[0] <= i < sum(g)][0]
        keys = [(k, group if k == 3 else i if (k, i) in self.mine else None) for k in rounds]
        self.result, theirs, self.token = last_gamma(
            self.token, self.place, i, self.terms(*keys), self.gamma, self.shape, self.result
        )
        self.received[i] = self.to_core(theirs)

    def put(self, i):
        self.result, self.token = place_gamma(self.token, self.place, i, self.received[i], self.result)

    def steps(self):
        steps = {
            "hop_1": self.hop_1, "hop_2": self.hop_2, "hop_3": self.hop_3, "keep_3": self.keep_3,
            "combine_0": functools.partial(self.combine, 0, send="send_0" not in ORDER), "send_0": functools.partial(self.send, 0),
            "combine_1": functools.partial(self.combine, 1, split=SPLIT_1), "combine_2": functools.partial(self.combine, 2, split=SPLIT_2),
            "receive_0": functools.partial(self.receive, 0), "receive_1": functools.partial(self.receive, 1),
            "receive_2": functools.partial(self.receive, 2),
            "gamma_0": functools.partial(self.add, 0), "gamma_1": functools.partial(self.add, 1),
            "gamma_2": functools.partial(self.add, 2), "gamma_01": functools.partial(self.add, 0, 1),
            "gamma_12": functools.partial(self.add, 1, 2), "gamma_012": functools.partial(self.add, 0, 1, 2),
        }
        for k in range(3):
            steps[f"chip_{k}"], steps[f"own_{k}"] = functools.partial(self.pass_on, k), functools.partial(self.own, k)
        added = "".join(name for name in ORDER if name.startswith("gamma"))
        rounds = [k for k in range(4) if str(k) not in added]
        for n, group in enumerate(GROUPS):
            steps[f"chip_3_{n}"], steps[f"own_3_{n}"] = functools.partial(self.pass_on, 3, group), functools.partial(self.own, 3, group)
            steps[f"combine_3_{n}"] = functools.partial(self.combine, 3, group)
        for i in range(self.half):
            steps[f"last_{i}"], steps[f"place_{i}"] = functools.partial(self.last_sum, i, rounds), functools.partial(self.put, i)
        return steps


def chain_device(b_occ_i, b_occ_j, eps_occ_i, eps_occ_j, eps_vir):
    chain = Chain(b_occ_i, b_occ_j, eps_occ_i, eps_occ_j, eps_vir)
    steps = chain.steps()
    for name in ORDER:
        steps[name]()
    return chain.result


def general_device(b_occ_i, b_occ_j, eps_occ_i, eps_occ_j, eps_vir):
    rows = b_occ_i.shape[1]
    own_energy = lax.dynamic_slice_in_dim(eps_vir, lax.axis_index("row") * rows, rows, 0)
    gathered = lax.all_gather(b_occ_j, "row", axis=1, tiled=True)
    partial_value = jnp.einsum("iap,jbp->jiab", b_occ_i, gathered, preferred_element_type=F32)
    totals = lax.psum(partial_value.astype(BF16), "col").astype(F32)
    denominator = (
        eps_occ_j[:, None, None, None]
        + eps_occ_i[None, :, None, None]
        - own_energy[None, None, :, None]
        - eps_vir[None, None, None, :]
    )
    held = (totals / denominator).astype(BF16)
    mirror = jnp.swapaxes(lax.all_to_all(held, "row", split_axis=3, concat_axis=2, tiled=True), 2, 3)
    combined = (2.0 * held.astype(F32) - mirror.astype(F32)).astype(BF16)
    return jnp.einsum("jiab,jbp->iap", combined, gathered, preferred_element_type=F32)


def solution(mesh):
    placed = (
        P("groups", "row", "col"),
        P("groups", "row", "col"),
        P("groups"),
        P("groups"),
        P("groups"),
    )
    chain = mesh.shape["row"] == 4 and mesh.shape["col"] == 4
    return jax.shard_map(
        chain_device if chain else general_device,
        mesh=mesh,
        in_specs=placed,
        out_specs=P("groups", "row", "col"),
        check_vma=False,
    )
```
